32 devices in a mesh: grp: 2 (over y), layer: 16 (over z, x, core).
Axes of the slice: x: 2, y: 2, z: 4, core: 2. Of those that a mesh axis runs over, the one named last changes fastest.
Arguments:
- residual: bfloat16 [2, 4096, 3584], P(None, ('grp', 'layer')), parts along dimension 1, may hold values from -6 to 6
- mlp_target: bfloat16 [2, 4096, 3584], P(None, ('grp', 'layer')), parts along dimension 1, may hold values from -6 to 6
- pre_acts: bfloat16 [2, 4096, 1, 128], P(None, ('grp', 'layer')), parts along dimension 1, may hold values from -6 to 6
- blocks: int32 [2, 4096, 1], P(None, ('grp', 'layer')), parts along dimension 1, may hold values from 0 to 15; in each aligned block of 128 rows (0 to 127, 128 to 255, ..., all dimensions but the last counted through in order) at most 16 rows name the same one
- decoder: bfloat16 [3, 2048, 3584], P(None, 'layer'), may hold values from -0.5 to 0.5
- decoder_bias: float32 [2, 3584], replicated, may hold values from -3 to 3
Outputs:
- decoder_gradient: bfloat16 [6, 2048, 3584], P('grp', 'layer'), parts along dimension 0
- encoder_gradient: bfloat16 [4, 3584, 2048], P('grp', None, 'layer'), parts along dimension 0
- encoder_bias_gradient: float32 [4, 2048], P('grp', 'layer'), parts along dimension 0
- decoder_bias_gradient: float32 [4, 3584], P('grp'), parts along dimension 0
The draws below stay inside these ranges and needn't reach their ends.
There are 2 independent parts, one for each index of `grp`. The reference program is written for one: setup_inputs(seed, part) draws one part's arguments, and reference() takes and returns one part's arrays. A program takes and returns all parts, laid end to end along the dimension named above; an argument that names none is the same for every part. Nothing has to cross between parts.
Inputs may be any that keep to these rules, and one draw needn't show every extreme that they name: Each row names 1 different blocks. Among the rows of one device in one layer (aligned blocks of 128 rows over the first two dimensions taken together) no block is named more than 16 times.
All inputs are finite; a program needn't handle non-finite values.
Results may differ from the reference program's by a relative error of at most 0.0051.
Values may be sent and summed in bfloat16 or wider, within the bound.
No kernel may reach another device: no remote copies, remote signals or barrier semaphores. Data moves between devices by JAX's collectives and lax.ppermute only.
A program may use at most 128 MiB of HBM per device.

```python
import math
import jax
import jax.numpy as jnp
import numpy as np
from jax import lax

D = 3584
BLK = 128
LAYERS = 2
TOPB = 1
TOK_DEV = 128
NBLK = 16
LATENTS = 2048
TOKENS = 2048
PAIRS = 3
CAP = 16
N_LAYER = 16


def shard_levels(rng, dims, split, least, high):
    factor_of, own = 1.0, jax.random.fold_in(rng, 6)
    for axis_at, blocks in split:
        draws = jnp.exp(jax.random.uniform(jax.random.fold_in(own, axis_at), (blocks,), jnp.float32, least / len(split), high / len(split)))
        factor_of = factor_of * jnp.repeat(draws, dims[axis_at] // blocks).reshape([-1 if axis == axis_at else 1 for axis in range(len(dims))])
    return factor_of


def routed_block(stream_key, own, number, rows, amount, top, bound, slope):
    order = jax.random.permutation(stream_key, amount)
    heavy_load, usual = shares(amount, rows * top, bound, slope, True), shares(amount, rows * top, bound, slope, False)
    places = jnp.arange(amount)

    def named(sizes, rotation):
        used = int((sizes > 0).sum())
        fixed = max(1, used // 4)
        passed = fixed + (places - fixed + rotation * (used - fixed)) % max(1, amount - fixed)
        return jnp.zeros((amount,), jnp.int32).at[order[jnp.where(places < fixed, places, passed)]].set(jnp.asarray(sizes, jnp.int32))

    sizes = jnp.where(number % 4 == 0, named(heavy_load, number // 4), named(usual, number - number // 4 - 1))
    mixed = jax.random.permutation(jax.random.fold_in(own, 3), amount)
    donor, receiver = mixed[0:amount // 2 * 2:2], mixed[1:amount // 2 * 2:2]
    margin = jnp.minimum(sizes[donor] - 1, bound - sizes[receiver]) // 2
    margin = jnp.where((donor == order[0]) | (receiver == order[0]) | (sizes[receiver] == 0), 0, jnp.maximum(margin, 0))
    passed = jax.random.randint(jax.random.fold_in(own, 4), (amount // 2,), 0, 1 << 20) % (margin + 1)
    sizes = sizes.at[donor].add(-passed).at[receiver].add(passed)
    members = jnp.searchsorted(jnp.cumsum(sizes), jnp.arange(rows * top), side="right").astype(jnp.int32)
    grid = members.reshape(top, rows).T
    grid = grid[jax.random.permutation(jax.random.fold_in(own, 1), rows)]
    rotation = jax.random.randint(jax.random.fold_in(own, 2), (rows, 1), 0, top)
    return jnp.take_along_axis(grid, (jnp.arange(top)[None, :] + rotation) % top, axis=1)


def shares(amount, total, most, lean, full):
    loads = [(1 << 20) // math.isqrt(grade ** lean) + 1 for grade in range(1, amount + 1)]
    largest = most if full else min(most, max(-(-total // amount), total * loads[0] // sum(loads)))
    least = 1 if total - largest >= amount - 1 else 0
    counts, rest = [largest] + [least] * (amount - 1), total - largest - least * (amount - 1)
    while rest > 0:
        movable = [i for i in range(1, amount) if counts[i] < largest] or [i for i in range(1, amount) if counts[i] < most]
        mass, remaining = sum([loads[i] for i in movable]), rest
        for i in movable:
            more = min(most - counts[i], max(1, remaining * loads[i] // mass), rest)
            counts[i] = counts[i] + more
            rest = rest - more
    return np.array(counts)


def scatter_about(key, extent, width, most, cuts=(), kind=jnp.bfloat16):
    values = width * jax.random.normal(key, extent, jnp.float32)
    if cuts:
        values = values * shard_levels(key, extent, cuts, -0.22, 0.18)
    return jnp.clip(values, -most, most).astype(kind)


def setup_inputs(seed: int = 0, part: int = 0) -> dict:
    streams_of = jax.random.split(jax.random.key(seed), 7)
    part_keys = jax.random.split(jax.random.fold_in(streams_of[6], part), 7)
    residual = scatter_about(part_keys[0], (LAYERS, TOKENS, D), 1.0, 6.0, ((1, 16),))
    mlp_target = scatter_about(part_keys[1], (LAYERS, TOKENS, D), 1.0, 6.0, ((1, 16),))
    pre_acts = scatter_about(part_keys[2], (LAYERS, TOKENS, TOPB, BLK), 1.0, 6.0, ((1, 16),))
    blocks_keys = jax.random.split(jax.random.fold_in(part_keys[3], 1), LAYERS * TOKENS // TOK_DEV)
    blocks_turns = jax.random.permutation(jax.random.fold_in(part_keys[3], 3), LAYERS * TOKENS // TOK_DEV)
    blocks = jax.vmap(lambda own, number: routed_block(jax.random.fold_in(part_keys[3], 2), own, number, TOK_DEV, NBLK, TOPB, CAP, 2))(blocks_keys, blocks_turns).reshape((LAYERS, TOKENS, TOPB))
    decoder = scatter_about(streams_of[4], (PAIRS, LATENTS, D), BLK ** -0.5, 0.5, ((1, 16),))
    decoder_bias = scatter_about(streams_of[5], (LAYERS, D), 0.5, 3.0, (), jnp.float32)
    return {"residual": residual, "mlp_target": mlp_target, "pre_acts": pre_acts, "blocks": blocks, "decoder": decoder, "decoder_bias": decoder_bias}


def pair_index(source, output_layer):
    return source * LAYERS - source * (source - 1) // 2 + (output_layer - source)

def slot_table(blocks):
    per_device = TOK_DEV * TOPB
    routes = blocks.reshape(LAYERS, N_LAYER, per_device).astype(jnp.int32)
    matches = (routes[:, :, :, None] == jnp.arange(NBLK, dtype=jnp.int32)).astype(jnp.int32)
    ordinal = lax.optimization_barrier(jnp.sum((jnp.cumsum(matches, axis=2) - 1) * matches, axis=3))
    sender = jnp.arange(N_LAYER, dtype=jnp.int32)[None, :, None]
    slot_of = (sender * CAP + ordinal).astype(jnp.int32)
    route_ids = jnp.broadcast_to(sender * per_device + jnp.arange(per_device, dtype=jnp.int32)[None, None, :], routes.shape)
    layer_ids = jnp.broadcast_to(jnp.arange(LAYERS, dtype=jnp.int32)[:, None, None], routes.shape)
    table = jnp.full((LAYERS, NBLK, N_LAYER * CAP), TOKENS * TOPB, jnp.int32)
    return table.at[layer_ids, routes, slot_of].set(route_ids.astype(jnp.int32))

def reference(residual, mlp_target, pre_acts, blocks, decoder, decoder_bias):
    err_scale = 1.0 / math.sqrt(TOK_DEV * TOPB)
    table = jnp.transpose(slot_table(blocks), (1, 0, 2))
    pre_rows = jnp.concatenate([pre_acts.reshape(LAYERS, TOKENS * TOPB, BLK), jnp.zeros((LAYERS, 1, BLK), pre_acts.dtype)], axis=1)
    resid_rows = jnp.concatenate([residual, jnp.zeros((LAYERS, 1, D), residual.dtype)], axis=1)
    dec_blocks = jnp.transpose(decoder.reshape(PAIRS, NBLK, BLK, D), (1, 0, 2, 3))

    def forward(rebuilt, inputs):
        slot_routes, dec_local = inputs
        for source in range(LAYERS):
            latent_act = jnp.maximum(pre_rows[source][slot_routes[source]], 0)
            token_ids = slot_routes[source] // TOPB
            for output_layer in range(source, LAYERS):
                contribution = jnp.dot(latent_act, dec_local[pair_index(source, output_layer)], preferred_element_type=jnp.float32)
                contribution = lax.optimization_barrier(contribution.astype(jnp.bfloat16)).astype(jnp.float32)
                rebuilt = rebuilt.at[output_layer, token_ids].add(contribution)
        return (rebuilt, None)
    rebuilt, _ = lax.scan(forward, jnp.zeros((LAYERS, TOKENS + 1, D), jnp.float32), (table, dec_blocks))
    summed = rebuilt[:, :TOKENS] + decoder_bias[:, None, :]
    errors = ((summed - mlp_target.astype(jnp.float32)) * err_scale).astype(jnp.bfloat16)
    decoder_bias_gradient = lax.optimization_barrier(jnp.sum(errors.astype(jnp.float32), axis=1))
    error_rows = jnp.concatenate([errors, jnp.zeros((LAYERS, 1, D), jnp.bfloat16)], axis=1)

    def backward(inputs):
        slot_routes, dec_local = inputs
        dec_grads = [None] * PAIRS
        enc_grads = []
        bias_grads = []
        for source in range(LAYERS):
            pre_local = pre_rows[source][slot_routes[source]]
            latent_act = jnp.maximum(pre_local, 0)
            token_ids = slot_routes[source] // TOPB
            resid_local = resid_rows[source][token_ids]
            latent_grad = jnp.zeros((N_LAYER * CAP, BLK), jnp.float32)
            for output_layer in range(source, LAYERS):
                pair_slot = pair_index(source, output_layer)
                error_local = error_rows[output_layer][token_ids]
                latent_grad = latent_grad + lax.dot_general(error_local, dec_local[pair_slot], (((1,), (1,)), ((), ())), preferred_element_type=jnp.float32)
                dec_grads[pair_slot] = lax.dot_general(latent_act, error_local, (((0,), (0,)), ((), ())), preferred_element_type=jnp.float32).astype(jnp.bfloat16)
            pre_grad = jnp.where(pre_local > 0, latent_grad, 0.0)
            bias_grads.append(lax.optimization_barrier(jnp.sum(pre_grad, axis=0)))
            enc_grads.append(lax.dot_general(resid_local, pre_grad.astype(jnp.bfloat16), (((0,), (0,)), ((), ())), preferred_element_type=jnp.float32).astype(jnp.bfloat16))
        return (jnp.stack(dec_grads), jnp.stack(enc_grads), jnp.stack(bias_grads))
    dec_all, enc_all, bias_all = lax.map(backward, (table, dec_blocks))
    decoder_gradient = jnp.transpose(dec_all, (1, 0, 2, 3)).reshape(PAIRS, LATENTS, D)
    encoder_gradient = jnp.transpose(enc_all, (1, 2, 0, 3)).reshape(LAYERS, D, LATENTS)
    encoder_bias_gradient = jnp.transpose(bias_all, (1, 0, 2)).reshape(LAYERS, LATENTS)
    return (decoder_gradient, encoder_gradient, encoder_bias_gradient, decoder_bias_gradient)
```

```python
import math

import jax
import jax.numpy as jnp
from jax import lax
from jax.sharding import PartitionSpec as P

BF = jnp.bfloat16
F32 = jnp.float32


def mm(a, b, dims=((1,), (0,))):
    return lax.dot_general(a, b, (dims, ((), ())), preferred_element_type=F32)


def per_device(residual, mlp_target, pre_acts, blocks, decoder, decoder_bias):
    devices = lax.axis_size("layer")
    layers, tokens, width = residual.shape
    latents = pre_acts.shape[3]
    cap = max(2, 2 * tokens // devices)
    slots = devices * cap
    scale = 1.0 / math.sqrt(tokens)

    def exchange(x):
        return lax.all_to_all(x, "layer", split_axis=0, concat_axis=0, tiled=True)

    routes = blocks.reshape(layers, tokens)
    earlier = jnp.arange(tokens)[:, None] > jnp.arange(tokens)[None, :]
    same = routes[:, :, None] == routes[:, None, :]
    ordinal = jnp.sum((same & earlier).astype(jnp.int32), axis=2)
    slot_of = routes * cap + ordinal
    place = (slot_of[:, None, :] == jnp.arange(slots, dtype=jnp.int32)[None, :, None]).astype(BF)
    place0, place1 = place[0], place[1]
    pre = pre_acts.reshape(layers, tokens, latents)

    first = jnp.concatenate(
        [
            mm(place0, mlp_target[0]).astype(BF),
            mm(place0, pre[0]).astype(BF),
            mm(place1, pre[1]).astype(BF),
        ],
        axis=1,
    )
    first = exchange(first.reshape(devices, cap, width + 2 * latents)).reshape(slots, -1)
    target_in, pre0, pre1 = (
        first[:, :width],
        first[:, width : width + latents],
        first[:, width + latents :],
    )
    act0, act1 = jnp.maximum(pre0, 0), jnp.maximum(pre1, 0)

    def pair_up(a, b):
        return jnp.concatenate(
            [a.reshape(devices, cap, width), b.reshape(devices, cap, width)], axis=1
        )

    def split_up(x):
        return x[:, :cap].reshape(slots, width), x[:, cap:].reshape(slots, width)

    pieces = exchange(
        pair_up(mm(act0, decoder[1]).astype(BF), mm(act1, decoder[2]).astype(BF))
    )
    resid_in = exchange(
        pair_up(mm(place0, residual[0]).astype(BF), mm(place1, residual[1]).astype(BF))
    )

    piece00 = mm(act0, decoder[0]).astype(BF).astype(F32)
    error0 = ((piece00 + decoder_bias[0] - target_in.astype(F32)) * scale).astype(BF)
    empty0 = (decoder_bias[0] * scale).astype(BF).astype(F32)
    empties = float(slots * devices - tokens * devices)

    back0, back1 = split_up(pieces)
    rebuilt = mm(place0, back0, ((0,), (0,))) + mm(place1, back1, ((0,), (0,))) + decoder_bias[1]
    error1 = ((rebuilt - mlp_target[1].astype(F32)) * scale).astype(BF)
    sums = jnp.stack(
        [jnp.sum(error0.astype(F32), axis=0), jnp.sum(error1.astype(F32), axis=0)]
    )
    sums = jnp.sum(lax.all_gather(sums, "layer"), axis=0)
    bias_grad = sums - jnp.stack([empties * empty0, jnp.zeros_like(empty0)])

    errors_in = exchange(
        pair_up(mm(place0, error1).astype(BF), mm(place1, error1).astype(BF))
    )
    error01, error11 = split_up(errors_in)
    resid0, resid1 = split_up(resid_in)

    grad0 = mm(error0, decoder[0], ((1,), (1,))) + mm(error01, decoder[1], ((1,), (1,)))
    grad1 = mm(error11, decoder[2], ((1,), (1,)))
    grad0 = jnp.where(pre0 > 0, grad0, 0.0)
    grad1 = jnp.where(pre1 > 0, grad1, 0.0)
    rows = ((0,), (0,))
    dec = jnp.stack(
        [
            mm(act0, error0, rows).astype(BF),
            mm(act0, error01, rows).astype(BF),
            mm(act1, error11, rows).astype(BF),
        ]
    )
    enc = jnp.stack(
        [
            mm(resid0, grad0.astype(BF), rows).astype(BF),
            mm(resid1, grad1.astype(BF), rows).astype(BF),
        ]
    )
    return dec, enc, jnp.stack([jnp.sum(grad0, axis=0), jnp.sum(grad1, axis=0)]), bias_grad


def solution(mesh):
    return jax.shard_map(
        per_device,
        mesh=mesh,
        in_specs=(
            P(None, ("grp", "layer"), None),
            P(None, ("grp", "layer"), None),
            P(None, ("grp", "layer"), None, None),
            P(None, ("grp", "layer"), None),
            P(None, "layer", None),
            P(),
        ),
        out_specs=(
            P("grp", "layer", None),
            P("grp", None, "layer"),
            P("grp", "layer"),
            P("grp", None),
        ),
        check_vma=False,
    )
```

```python
import math

import jax
import jax.numpy as jnp
from jax import lax
from jax.sharding import PartitionSpec as P

BF = jnp.bfloat16
F32 = jnp.float32
ROWS = ((0,), (0,))
LAST = ((1,), (1,))


def mm(a, b, dims=((1,), (0,))):
    return lax.dot_general(a, b, (dims, ((), ())), preferred_element_type=F32)


def per_device(residual, mlp_target, pre_acts, blocks, decoder, decoder_bias):
    devices = lax.axis_size("layer")
    layers, tokens, width = residual.shape
    latents = pre_acts.shape[3]
    cap = max(2, 2 * tokens // devices)
    slots = devices * cap
    half = devices // 2
    scale = 1.0 / math.sqrt(tokens)
    me = lax.axis_index("layer")
    upper = me >= half
    mirror = [(i, (i + half) % devices) for i in range(devices)]
    halves = [list(range(half)), list(range(half, devices))]

    def everyone(x):
        return lax.all_to_all(x, "layer", split_axis=0, concat_axis=0, tiled=True)

    def within(x):
        return lax.all_to_all(
            x, "layer", split_axis=0, concat_axis=0, tiled=True, axis_index_groups=halves
        )

    def across(x):
        return lax.ppermute(x, "layer", mirror)

    def turn(x):
        first, second = x[: x.shape[0] // 2], x[x.shape[0] // 2 :]
        return jnp.concatenate(
            [jnp.where(upper, second, first), jnp.where(upper, first, second)], axis=0
        )

    routes = blocks.reshape(layers, tokens)
    earlier = jnp.arange(tokens)[:, None] > jnp.arange(tokens)[None, :]

    def ordinals(named):
        same = named[:, :, None] == named[:, None, :]
        return jnp.sum((same & earlier).astype(jnp.int32), axis=2)

    routes_m = across(routes)
    pre = pre_acts.reshape(layers, tokens, latents)
    resid1_m = across(residual[1])

    order = ordinals(routes)
    slot_of = routes * cap + order
    place = (slot_of[:, None, :] == jnp.arange(slots, dtype=jnp.int32)[None, :, None]).astype(BF)

    def pair_places(named, order, base):
        block = base + jnp.arange(half, dtype=jnp.int32)[:, None, None, None]
        slot = jnp.arange(cap, dtype=jnp.int32)[None, None, :, None]
        hit = (named[None, :, None, :] == block) & (order[None, :, None, :] == slot)
        return hit.astype(BF).reshape(half, layers, cap, tokens)

    base = jnp.where(upper, half, 0).astype(jnp.int32)
    place_o = pair_places(routes, order, base)
    place_m = pair_places(routes_m, ordinals(routes_m), base)

    def flat(p):
        return p.reshape(-1, p.shape[-1])

    sent_pre = jnp.stack(
        [mm(place[l], pre[l]).astype(BF).reshape(devices, cap, latents) for l in range(layers)],
        axis=1,
    )
    got_pre = everyone(sent_pre.reshape(devices, layers * cap, latents))
    got_pre = got_pre.reshape(devices, layers, cap, latents)
    pre0 = got_pre[:, 0].reshape(slots, latents)
    pre1 = got_pre[:, 1].reshape(slots, latents)
    act0 = jnp.maximum(pre0, 0)

    acts = turn(jnp.maximum(got_pre, 0))
    nothing = jnp.zeros((devices, 1, cap, latents), BF)
    wide = jnp.concatenate(
        [
            jnp.concatenate([acts[:, 0:1], nothing], axis=3),
            jnp.concatenate([nothing, acts[:, 1:2]], axis=3),
        ],
        axis=1,
    ).reshape(devices, layers * cap, 2 * latents)
    dec1 = decoder[1:3].reshape(2 * latents, width)

    def decode(rows):
        return mm(rows.reshape(-1, 2 * latents), dec1).astype(BF).reshape(half, -1, width)

    pieces_m = within(decode(wide[half:])).reshape(-1, width)
    sum_m = mm(flat(place_m), pieces_m, ROWS)
    sum_low = across(sum_m.astype(BF))
    pieces_o = within(decode(wide[:half])).reshape(-1, width)
    sum_o = mm(flat(place_o), pieces_o, ROWS) + decoder_bias[1] - mlp_target[1].astype(F32)
    sum_high = across(sum_o.astype(BF))

    error1 = ((sum_o + sum_low.astype(F32)) * scale).astype(BF)
    error1_m = ((sum_m + sum_high.astype(F32)) * scale).astype(BF)

    def send_errors(p, error):
        return within(mm(flat(p), error).astype(BF).reshape(half, layers * cap, width))

    resid1_in = within(
        jnp.concatenate(
            [
                mm(flat(place_o[:, 1]), residual[1]).astype(BF).reshape(half, cap, width),
                mm(flat(place_m[:, 1]), resid1_m).astype(BF).reshape(half, cap, width),
            ],
            axis=1,
        )
    )
    errors_o = send_errors(place_o, error1)
    errors_m = send_errors(place_m, error1_m)

    layer0 = everyone(
        jnp.concatenate(
            [
                mm(place[0], mlp_target[0]).astype(BF).reshape(devices, cap, width),
                mm(place[0], residual[0]).astype(BF).reshape(devices, cap, width),
            ],
            axis=1,
        )
    )
    target0 = layer0[:, :cap].reshape(slots, width)
    resid0 = layer0[:, cap:].reshape(slots, width)
    piece00 = mm(act0, decoder[0]).astype(BF).astype(F32)
    error0 = ((piece00 + decoder_bias[0] - target0.astype(F32)) * scale).astype(BF)
    empty0 = (decoder_bias[0] * scale).astype(BF).astype(F32)
    empties = float(slots * devices - tokens * devices)

    def total(x):
        step = 1
        while step < devices:
            x = x + lax.ppermute(x, "layer", [(i, i ^ step) for i in range(devices)])
            step *= 2
        return x

    bias_grad = jnp.stack(
        [
            total(jnp.sum(error0.astype(F32), axis=0)[None])[0] - empties * empty0,
            total(jnp.sum(error1.astype(F32), axis=0)[None])[0],
        ]
    )

    wide_o = wide[:half].reshape(-1, 2 * latents)
    wide_m = wide[half:].reshape(-1, 2 * latents)
    errors_o = errors_o.reshape(-1, width)
    errors_m = errors_m.reshape(-1, width)
    dec_later = mm(wide_o, errors_o, ROWS) + mm(wide_m, errors_m, ROWS)
    back = jnp.concatenate([mm(errors_o, dec1, LAST), mm(errors_m, dec1, LAST)], axis=0)
    back = back.reshape(devices, layers, cap, 2 * latents)
    pres = turn(got_pre)
    grad1 = jnp.where(pres[:, 1] > 0, back[:, 1, :, latents:], 0.0)
    grad0 = turn(back[:, 0, :, :latents]).reshape(slots, latents) + mm(error0, decoder[0], LAST)
    grad0 = jnp.where(pre0 > 0, grad0, 0.0)
    low1 = grad1.astype(BF).reshape(2, half, cap, latents).swapaxes(0, 1).reshape(slots, latents)
    dec = jnp.concatenate(
        [mm(act0, error0, ROWS).astype(BF)[None], dec_later.astype(BF).reshape(2, latents, width)]
    )
    enc = jnp.stack(
        [
            mm(resid0, grad0.astype(BF), ROWS).astype(BF),
            mm(resid1_in.reshape(slots, width), low1, ROWS).astype(BF),
        ]
    )
    enc_bias = jnp.stack([jnp.sum(grad0, axis=0), jnp.sum(grad1, axis=(0, 1))])
    return dec, enc, enc_bias, bias_grad


def solution(mesh):
    return jax.shard_map(
        per_device,
        mesh=mesh,
        in_specs=(
            P(None, ("grp", "layer"), None),
            P(None, ("grp", "layer"), None),
            P(None, ("grp", "layer"), None, None),
            P(None, ("grp", "layer"), None),
            P(None, "layer", None),
            P(),
        ),
        out_specs=(
            P("grp", "layer", None),
            P("grp", None, "layer"),
            P("grp", "layer"),
            P("grp", None),
        ),
        check_vma=False,
    )
```

```python
import math

import jax
import jax.numpy as jnp
from jax import lax
from jax.sharding import PartitionSpec as P

BF = jnp.bfloat16
F32 = jnp.float32
ROWS = ((0,), (0,))
LAST = ((1,), (1,))


def mm(a, b, dims=((1,), (0,))):
    return lax.dot_general(a, b, (dims, ((), ())), preferred_element_type=F32)


def per_device(residual, mlp_target, pre_acts, blocks, decoder, decoder_bias):
    devices = lax.axis_size("layer")
    layers, tokens, width = residual.shape
    latents = pre_acts.shape[3]
    cap = max(2, 2 * tokens // devices)
    slots = devices * cap
    half = devices // 2
    scale = 1.0 / math.sqrt(tokens)
    me = lax.axis_index("layer")
    upper = me >= half
    mirror = [(i, (i + half) % devices) for i in range(devices)]
    halves = [list(range(half)), list(range(half, devices))]

    def everyone(x):
        return lax.all_to_all(x, "layer", split_axis=0, concat_axis=0, tiled=True)

    def within(x):
        return lax.all_to_all(
            x, "layer", split_axis=0, concat_axis=0, tiled=True, axis_index_groups=halves
        )

    def after(x, done):
        return lax.optimization_barrier((x, done))[0]

    def across(x):
        return lax.ppermute(x, "layer", mirror)

    def turn(x):
        first, second = x[: x.shape[0] // 2], x[x.shape[0] // 2 :]
        return jnp.concatenate(
            [jnp.where(upper, second, first), jnp.where(upper, first, second)], axis=0
        )

    routes = blocks.reshape(layers, tokens)
    earlier = jnp.arange(tokens)[:, None] > jnp.arange(tokens)[None, :]

    def ordinals(named):
        same = named[:, :, None] == named[:, None, :]
        return jnp.sum((same & earlier).astype(jnp.int32), axis=2)

    pre = pre_acts.reshape(layers, tokens, latents)
    resid1_m = across(residual[1])

    order = ordinals(routes)
    routes_m, order_m = across(jnp.stack([routes, order]))
    slot_of = routes * cap + order
    place = (slot_of[:, None, :] == jnp.arange(slots, dtype=jnp.int32)[None, :, None]).astype(BF)

    def pair_places(named, order, base):
        block = base + jnp.arange(half, dtype=jnp.int32)[:, None, None, None]
        slot = jnp.arange(cap, dtype=jnp.int32)[None, None, :, None]
        hit = (named[None, :, None, :] == block) & (order[None, :, None, :] == slot)
        return hit.astype(BF).reshape(half, layers, cap, tokens)

    base = jnp.where(upper, half, 0).astype(jnp.int32)
    place_o = pair_places(routes, order, base)
    place_m = pair_places(routes_m, order_m, base)

    def flat(p):
        return p.reshape(-1, p.shape[-1])

    sent_pre = jnp.stack(
        [mm(place[l], pre[l]).astype(BF).reshape(devices, cap, latents) for l in range(layers)],
        axis=1,
    )
    got_pre = everyone(sent_pre.reshape(devices, layers * cap, latents))
    got_pre = got_pre.reshape(devices, layers, cap, latents)
    pre0 = got_pre[:, 0].reshape(slots, latents)
    pre1 = got_pre[:, 1].reshape(slots, latents)
    act0 = jnp.maximum(pre0, 0)

    acts = turn(jnp.maximum(got_pre, 0))
    nothing = jnp.zeros((devices, 1, cap, latents), BF)
    wide = jnp.concatenate(
        [
            jnp.concatenate([acts[:, 0:1], nothing], axis=3),
            jnp.concatenate([nothing, acts[:, 1:2]], axis=3),
        ],
        axis=1,
    ).reshape(devices, layers * cap, 2 * latents)
    dec1 = decoder[1:3].reshape(2 * latents, width)

    def decode(rows):
        return mm(rows.reshape(-1, 2 * latents), dec1).astype(BF).reshape(half, -1, width)

    pieces_m = within(decode(wide[half:])).reshape(-1, width)
    sum_m = mm(flat(place_m), pieces_m, ROWS)
    sum_low_sent = sum_m.astype(BF)
    sum_low = across(sum_low_sent)
    pieces_o = within(decode(after(wide[:half], sum_low_sent))).reshape(-1, width)
    sum_o = mm(flat(place_o), pieces_o, ROWS) + decoder_bias[1] - mlp_target[1].astype(F32)
    sum_high_sent = sum_o.astype(BF)
    sum_high = across(sum_high_sent)

    error1 = ((sum_o + sum_low.astype(F32)) * scale).astype(BF)
    error1_m = ((sum_m + sum_high.astype(F32)) * scale).astype(BF)

    def send_errors(p, error):
        return within(mm(flat(p), error).astype(BF).reshape(half, layers * cap, width))

    residual1 = after(residual[1], sum_high_sent)
    resid1_in = within(
        jnp.concatenate(
            [
                mm(flat(place_o[:, 1]), residual1).astype(BF).reshape(half, cap, width),
                mm(flat(place_m[:, 1]), resid1_m).astype(BF).reshape(half, cap, width),
            ],
            axis=1,
        )
    )
    errors_o = send_errors(place_o, after(error1, resid1_in))
    errors_m = send_errors(place_m, after(error1_m, errors_o))

    target_last = after(mlp_target[0], errors_m)
    target0 = everyone(mm(place[0], target_last).astype(BF).reshape(devices, cap, width))
    residual_last = after(residual[0], target0)
    resid0 = everyone(mm(place[0], residual_last).astype(BF).reshape(devices, cap, width))
    target0, resid0 = target0.reshape(slots, width), resid0.reshape(slots, width)
    piece00 = mm(act0, decoder[0]).astype(BF).astype(F32)
    error0 = ((piece00 + decoder_bias[0] - target0.astype(F32)) * scale).astype(BF)
    empty0 = (decoder_bias[0] * scale).astype(BF).astype(F32)
    empties = float(slots * devices - tokens * devices)

    def total(x):
        step = 1
        while step < devices:
            x = x + lax.ppermute(x, "layer", [(i, i ^ step) for i in range(devices)])
            step *= 2
        return x

    sums = total(
        jnp.stack([jnp.sum(error0.astype(F32), axis=0), jnp.sum(error1.astype(F32), axis=0)])
    )
    bias_grad = sums - jnp.stack([empties * empty0, jnp.zeros_like(empty0)])

    wide_o = wide[:half].reshape(-1, 2 * latents)
    wide_m = wide[half:].reshape(-1, 2 * latents)
    errors_o = errors_o.reshape(-1, width)
    errors_m = errors_m.reshape(-1, width)
    dec_later = mm(wide_o, errors_o, ROWS) + mm(wide_m, errors_m, ROWS)
    back = jnp.concatenate([mm(errors_o, dec1, LAST), mm(errors_m, dec1, LAST)], axis=0)
    back = back.reshape(devices, layers, cap, 2 * latents)
    pres = turn(got_pre)
    grad1 = jnp.where(pres[:, 1] > 0, back[:, 1, :, latents:], 0.0)
    grad0 = turn(back[:, 0, :, :latents]).reshape(slots, latents) + mm(error0, decoder[0], LAST)
    grad0 = jnp.where(pre0 > 0, grad0, 0.0)
    low1 = grad1.astype(BF).reshape(2, half, cap, latents).swapaxes(0, 1).reshape(slots, latents)
    dec = jnp.concatenate(
        [mm(act0, error0, ROWS).astype(BF)[None], dec_later.astype(BF).reshape(2, latents, width)]
    )
    enc = jnp.stack(
        [
            mm(resid0, grad0.astype(BF), ROWS).astype(BF),
            mm(resid1_in.reshape(slots, width), low1, ROWS).astype(BF),
        ]
    )
    enc_bias = jnp.stack([jnp.sum(grad0, axis=0), jnp.sum(grad1, axis=(0, 1))])
    return dec, enc, enc_bias, bias_grad


def solution(mesh):
    return jax.shard_map(
        per_device,
        mesh=mesh,
        in_specs=(
            P(None, ("grp", "layer"), None),
            P(None, ("grp", "layer"), None),
            P(None, ("grp", "layer"), None, None),
            P(None, ("grp", "layer"), None),
            P(None, "layer", None),
            P(),
        ),
        out_specs=(
            P("grp", "layer", None),
            P("grp", None, "layer"),
            P("grp", "layer"),
            P("grp", None),
        ),
        check_vma=False,
    )
```

```python
import math

import jax
import jax.numpy as jnp
from jax import lax
from jax.experimental import pallas as pl
from jax.experimental.pallas import tpu as pltpu
from jax.sharding import PartitionSpec as P

BF = jnp.bfloat16
F32 = jnp.float32
ROWS = ((0,), (0,))
LAST = ((1,), (1,))


def mm(a, b, dims=((1,), (0,))):
    return lax.dot_general(a, b, (dims, ((), ())), preferred_element_type=F32)


def column_block(width):
    return next((b for b in (512, 256, 128) if width % b == 0), width)


def pack_rows(keys, rows, groups, cap):
    layers, tokens, width = rows.shape
    step = column_block(width)

    def kernel(keys_ref, rows_ref, *outs):
        slot = lax.broadcasted_iota(jnp.int32, (groups * cap, tokens), 0)
        for l in range(layers):
            hot = (keys_ref[l : l + 1, :] == slot).astype(F32).astype(BF)
            placed = mm(hot, rows_ref[l]).astype(BF)
            for k in range(groups):
                outs[k][l * cap : (l + 1) * cap, :] = placed[k * cap : (k + 1) * cap]

    return pl.pallas_call(
        kernel,
        grid=(width // step,),
        in_specs=[
            pl.BlockSpec((layers, tokens), lambda i: (0, 0)),
            pl.BlockSpec((layers, tokens, step), lambda i: (0, 0, i)),
        ],
        out_specs=[pl.BlockSpec((layers * cap, step), lambda i: (0, i))] * groups,
        out_shape=[jax.ShapeDtypeStruct((layers * cap, width), BF)] * groups,
        compiler_params=pltpu.CompilerParams(vmem_limit_bytes=32 * 2**20),
        cost_estimate=pl.CostEstimate(
            flops=2 * layers * groups * cap * tokens * width,
            bytes_accessed=2 * layers * (tokens + groups * cap) * width,
            transcendentals=0,
        ),
    )(keys, rows)


def encoder_products(rows, low, cap):
    layers, slots, latents = low.shape
    groups = len(rows)
    width = rows[0].shape[1]
    step = column_block(width)

    def kernel(low_ref, *refs):
        ins, out_ref, all_rows = refs[:groups], refs[groups], refs[groups + 1]
        for l in range(layers):
            for k in range(groups):
                all_rows[k * cap : (k + 1) * cap, :] = ins[k][l * cap : (l + 1) * cap, :]
            out_ref[l] = mm(all_rows[...], low_ref[l], ROWS).astype(BF)

    return pl.pallas_call(
        kernel,
        grid=(width // step,),
        in_specs=[pl.BlockSpec((layers, slots, latents), lambda i: (0, 0, 0))]
        + [pl.BlockSpec((layers * cap, step), lambda i: (0, i))] * groups,
        out_specs=pl.BlockSpec((layers, step, latents), lambda i: (0, i, 0)),
        out_shape=jax.ShapeDtypeStruct((layers, width, latents), BF),
        scratch_shapes=[pltpu.VMEM((slots, step), BF)],
        compiler_params=pltpu.CompilerParams(vmem_limit_bytes=32 * 2**20),
        cost_estimate=pl.CostEstimate(
            flops=2 * layers * slots * latents * width,
            bytes_accessed=2 * layers * (slots + latents) * width,
            transcendentals=0,
        ),
    )(low, *rows)


def per_device(residual, mlp_target, pre_acts, blocks, decoder, decoder_bias):
    devices = lax.axis_size("layer")
    layers, tokens, width = residual.shape
    latents = pre_acts.shape[3]
    cap = max(2, 2 * tokens // devices)
    slots = devices * cap
    half = devices // 2
    scale = 1.0 / math.sqrt(tokens)
    me = lax.axis_index("layer")
    upper = me >= half
    mirror = [(i, (i + half) % devices) for i in range(devices)]
    halves = [list(range(half)), list(range(half, devices))]

    def everyone(x):
        return lax.all_to_all(x, "layer", split_axis=0, concat_axis=0, tiled=True)

    def within(x):
        return lax.all_to_all(
            x, "layer", split_axis=0, concat_axis=0, tiled=True, axis_index_groups=halves
        )

    def after(x, done):
        return lax.optimization_barrier((x, done))[0]

    def across(x):
        return lax.ppermute(x, "layer", mirror)

    def turn(x):
        first, second = x[: x.shape[0] // 2], x[x.shape[0] // 2 :]
        return jnp.concatenate(
            [jnp.where(upper, second, first), jnp.where(upper, first, second)], axis=0
        )

    routes = blocks.reshape(layers, tokens)
    earlier = jnp.arange(tokens)[:, None] > jnp.arange(tokens)[None, :]

    def ordinals(named):
        same = named[:, :, None] == named[:, None, :]
        return jnp.sum((same & earlier).astype(jnp.int32), axis=2)

    pre = pre_acts.reshape(layers, tokens, latents)

    order = ordinals(routes)
    routes_m, order_m = across(jnp.stack([routes, order]))
    slot_of = routes * cap + order
    place = (slot_of[:, None, :] == jnp.arange(slots, dtype=jnp.int32)[None, :, None]).astype(BF)

    def pair_places(named, order, base):
        block = base + jnp.arange(half, dtype=jnp.int32)[:, None, None, None]
        slot = jnp.arange(cap, dtype=jnp.int32)[None, None, :, None]
        hit = (named[None, :, None, :] == block) & (order[None, :, None, :] == slot)
        return hit.astype(BF).reshape(half, layers, cap, tokens)

    base = jnp.where(upper, half, 0).astype(jnp.int32)
    place_o = pair_places(routes, order, base)
    place_m = pair_places(routes_m, order_m, base)

    def flat(p):
        return p.reshape(-1, p.shape[-1])

    sent_pre = jnp.stack(
        [mm(place[l], pre[l]).astype(BF).reshape(devices, cap, latents) for l in range(layers)],
        axis=1,
    )
    got_pre = everyone(sent_pre.reshape(devices, layers * cap, latents))
    got_pre = got_pre.reshape(devices, layers, cap, latents)
    pre0 = got_pre[:, 0].reshape(slots, latents)
    pre1 = got_pre[:, 1].reshape(slots, latents)
    act0 = jnp.maximum(pre0, 0)

    direct = devices <= 16 and cap % 16 == 0
    if direct:
        packed = pack_rows((routes ^ me) * cap + order, residual, devices, cap)
        resid_in = [packed[0]] + [
            lax.ppermute(packed[k], "layer", [(i, i ^ k) for i in range(devices)])
            for k in range(1, devices)
        ]
        early = [k for k in range(half, devices) if 8 * (k - half) < 3 * half]
        within_half = list(range(1, half))
        arrived = (me ^ jnp.arange(devices, dtype=jnp.int32)).astype(jnp.int32)
    else:
        resid_in = everyone(
            jnp.stack(
                [
                    mm(place[l], residual[l]).astype(BF).reshape(devices, cap, width)
                    for l in range(layers)
                ],
                axis=1,
            ).reshape(devices, layers * cap, width)
        )
        early, within_half = [], []

    def received(ks):
        return [resid_in[k] for k in ks]

    acts = turn(jnp.maximum(got_pre, 0))
    nothing = jnp.zeros((devices, 1, cap, latents), BF)
    wide = jnp.concatenate(
        [
            jnp.concatenate([acts[:, 0:1], nothing], axis=3),
            jnp.concatenate([nothing, acts[:, 1:2]], axis=3),
        ],
        axis=1,
    ).reshape(devices, layers * cap, 2 * latents)
    dec1 = decoder[1:3].reshape(2 * latents, width)

    def decode(rows):
        return mm(rows.reshape(-1, 2 * latents), dec1).astype(BF).reshape(half, -1, width)

    pieces_m = within(decode(wide[half:])).reshape(-1, width)
    sum_m = mm(flat(place_m), pieces_m, ROWS)
    sum_low_sent = sum_m.astype(BF)
    sum_low = across(sum_low_sent)
    pieces_o = within(decode(after(wide[:half], (sum_low_sent, received(early))))).reshape(-1, width)
    sum_o = mm(flat(place_o), pieces_o, ROWS) + decoder_bias[1] - mlp_target[1].astype(F32)
    sum_high_sent = sum_o.astype(BF)
    sum_high = across(sum_high_sent)

    error1 = ((sum_o + sum_low.astype(F32)) * scale).astype(BF)
    error1_m = ((sum_m + sum_high.astype(F32)) * scale).astype(BF)

    def send_errors(p, error):
        return within(mm(flat(p), error).astype(BF).reshape(half, layers * cap, width))

    error1 = after(error1, received(within_half[: half // 2]))
    errors_o = send_errors(place_o, error1)

    target_last = after(mlp_target[0], (errors_o, sum_high, received(within_half[half // 2 :])))
    target0 = everyone(mm(place[0], target_last).astype(BF).reshape(devices, cap, width))
    target0 = target0.reshape(slots, width)
    errors_m = send_errors(place_m, after(error1_m, target0))
    piece00 = mm(act0, decoder[0]).astype(BF).astype(F32)
    error0 = ((piece00 + decoder_bias[0] - target0.astype(F32)) * scale).astype(BF)
    empty0 = (decoder_bias[0] * scale).astype(BF).astype(F32)
    empties = float(slots * devices - tokens * devices)

    def total(x):
        step = 1
        while step < devices:
            x = x + lax.ppermute(x, "layer", [(i, i ^ step) for i in range(devices)])
            step *= 2
        return x

    sums = total(
        jnp.stack([jnp.sum(error0.astype(F32), axis=0), jnp.sum(error1.astype(F32), axis=0)])
    )
    bias_grad = sums - jnp.stack([empties * empty0, jnp.zeros_like(empty0)])

    wide_o = wide[:half].reshape(-1, 2 * latents)
    wide_m = wide[half:].reshape(-1, 2 * latents)
    errors_o = errors_o.reshape(-1, width)
    errors_m = errors_m.reshape(-1, width)
    dec_later = mm(wide_o, errors_o, ROWS) + mm(wide_m, errors_m, ROWS)
    back = jnp.concatenate([mm(errors_o, dec1, LAST), mm(errors_m, dec1, LAST)], axis=0)
    back = back.reshape(devices, layers, cap, 2 * latents)
    back = turn(back)
    own = mm(error0, decoder[0], LAST).reshape(devices, cap, latents)
    grads = jnp.stack([back[:, 0, :, :latents] + own, back[:, 1, :, latents:]], axis=1)
    grads = jnp.where(got_pre > 0, grads, 0.0)
    enc_bias = jnp.sum(grads, axis=(0, 2))
    low = grads.astype(BF)
    if direct:
        low = jnp.take(low, arrived, axis=0)
        low = jnp.swapaxes(low, 0, 1).reshape(layers, slots, latents)
        enc = encoder_products(resid_in, low, cap)
    else:
        low = jnp.swapaxes(low, 0, 1).reshape(layers, slots, latents)
        resid = resid_in.reshape(devices, layers, cap, width)
        resid = jnp.swapaxes(resid, 0, 1).reshape(layers, slots, width)
        enc = jnp.stack([mm(resid[l], low[l], ROWS).astype(BF) for l in range(layers)])
    dec = jnp.concatenate(
        [mm(act0, error0, ROWS).astype(BF)[None], dec_later.astype(BF).reshape(2, latents, width)]
    )
    return dec, enc, enc_bias, bias_grad


def solution(mesh):
    return jax.shard_map(
        per_device,
        mesh=mesh,
        in_specs=(
            P(None, ("grp", "layer"), None),
            P(None, ("grp", "layer"), None),
            P(None, ("grp", "layer"), None, None),
            P(None, ("grp", "layer"), None),
            P(None, "layer", None),
            P(),
        ),
        out_specs=(
            P("grp", "layer", None),
            P("grp", None, "layer"),
            P("grp", "layer"),
            P("grp", None),
        ),
        check_vma=False,
    )
```

```python
import math

import jax
import jax.numpy as jnp
from jax import lax
from jax.experimental import pallas as pl
from jax.experimental.pallas import tpu as pltpu
from jax.sharding import PartitionSpec as P

BF = jnp.bfloat16
F32 = jnp.float32
ROWS = ((0,), (0,))
LAST = ((1,), (1,))


def mm(a, b, dims=((1,), (0,))):
    return lax.dot_general(a, b, (dims, ((), ())), preferred_element_type=F32)


def column_block(width):
    return next((b for b in (512, 256, 128) if width % b == 0), width)


def pack_rows(key, first, second, groups, cap):
    _, tokens, width = first.shape
    step = column_block(width)

    def kernel(key_ref, first_ref, second_ref, *outs):
        slot = lax.broadcasted_iota(jnp.int32, (groups * cap, tokens), 0)
        hot = (key_ref[...] == slot).astype(F32).astype(BF)
        for at, rows_ref in enumerate((first_ref, second_ref)):
            placed = mm(hot, rows_ref[0]).astype(BF)
            for k in range(groups):
                outs[k][at * cap : (at + 1) * cap, :] = placed[k * cap : (k + 1) * cap]

    rows_spec = pl.BlockSpec((1, tokens, step), lambda i: (0, 0, i))
    return pl.pallas_call(
        kernel,
        grid=(width // step,),
        in_specs=[pl.BlockSpec((1, tokens), lambda i: (0, 0)), rows_spec, rows_spec],
        out_specs=[pl.BlockSpec((2 * cap, step), lambda i: (0, i))] * groups,
        out_shape=[jax.ShapeDtypeStruct((2 * cap, width), BF)] * groups,
        compiler_params=pltpu.CompilerParams(vmem_limit_bytes=32 * 2**20),
        cost_estimate=pl.CostEstimate(
            flops=4 * groups * cap * tokens * width,
            bytes_accessed=4 * (tokens + groups * cap) * width,
            transcendentals=0,
        ),
    )(key, first, second)


def per_device(residual, mlp_target, pre_acts, blocks, decoder, decoder_bias):
    devices = lax.axis_size("layer")
    layers, tokens, width = residual.shape
    latents = pre_acts.shape[3]
    cap = max(2, 2 * tokens // devices)
    slots = devices * cap
    half = devices // 2
    scale = 1.0 / math.sqrt(tokens)
    me = lax.axis_index("layer")
    upper = me >= half
    mirror = [(i, (i + half) % devices) for i in range(devices)]
    halves = [list(range(half)), list(range(half, devices))]

    def everyone(x):
        return lax.all_to_all(x, "layer", split_axis=0, concat_axis=0, tiled=True)

    def within(x):
        return lax.all_to_all(
            x, "layer", split_axis=0, concat_axis=0, tiled=True, axis_index_groups=halves
        )

    def after(x, done):
        return lax.optimization_barrier((x, done))[0]

    def across(x):
        return lax.ppermute(x, "layer", mirror)

    def turn(x):
        first, second = x[: x.shape[0] // 2], x[x.shape[0] // 2 :]
        return jnp.concatenate(
            [jnp.where(upper, second, first), jnp.where(upper, first, second)], axis=0
        )

    routes = blocks.reshape(layers, tokens)
    earlier = jnp.arange(tokens)[:, None] > jnp.arange(tokens)[None, :]

    def ordinals(named):
        same = named[:, :, None] == named[:, None, :]
        return jnp.sum((same & earlier).astype(jnp.int32), axis=2)

    pre = pre_acts.reshape(layers, tokens, latents)

    order = ordinals(routes)
    routes_m, order_m = across(jnp.stack([routes, order]))
    slot_of = routes * cap + order
    place = (slot_of[:, None, :] == jnp.arange(slots, dtype=jnp.int32)[None, :, None]).astype(BF)

    def pair_places(named, order, base):
        block = base + jnp.arange(half, dtype=jnp.int32)[:, None, None, None]
        slot = jnp.arange(cap, dtype=jnp.int32)[None, None, :, None]
        hit = (named[None, :, None, :] == block) & (order[None, :, None, :] == slot)
        return hit.astype(BF).reshape(half, layers, cap, tokens)

    base = jnp.where(upper, half, 0).astype(jnp.int32)
    place_o = pair_places(routes, order, base)
    place_m = pair_places(routes_m, order_m, base)

    def flat(p):
        return p.reshape(-1, p.shape[-1])

    sent_pre = jnp.stack(
        [mm(place[l], pre[l]).astype(BF).reshape(devices, cap, latents) for l in range(layers)],
        axis=1,
    )
    got_pre = everyone(sent_pre.reshape(devices, layers * cap, latents))
    got_pre = got_pre.reshape(devices, layers, cap, latents)
    direct = devices <= 16 and cap % 16 == 0
    if direct:
        key = ((routes[:1] ^ me) * cap + order[:1]).astype(jnp.int32)
        packed = pack_rows(key, mlp_target, residual, devices, cap)
        arrivals = [packed[0]] + [
            lax.ppermute(packed[k], "layer", [(i, i ^ k) for i in range(devices)])
            for k in range(1, devices)
        ]
        windows = [[8, 9, 10], [1, 4, 5], [2, 6], [3, 7, 11, 12, 13, 14, 15]]
        windows = [[k for k in ks if k < devices] for ks in windows]
        sender = (me ^ jnp.arange(devices, dtype=jnp.int32)).astype(jnp.int32)
    else:
        arrivals = [
            everyone(
                jnp.concatenate(
                    [
                        mm(place[0], rows[0]).astype(BF).reshape(devices, cap, width)
                        for rows in (mlp_target, residual)
                    ],
                    axis=1,
                )
            )
        ]
        windows = [[], [], [], [0]]

    def received(window):
        return [arrivals[k] for k in windows[window]]

    acts = turn(jnp.maximum(got_pre, 0))
    nothing = jnp.zeros((devices, 1, cap, latents), BF)
    wide = jnp.concatenate(
        [
            jnp.concatenate([acts[:, 0:1], nothing], axis=3),
            jnp.concatenate([nothing, acts[:, 1:2]], axis=3),
        ],
        axis=1,
    ).reshape(devices, layers * cap, 2 * latents)
    dec1 = decoder[1:3].reshape(2 * latents, width)

    def decode(rows):
        return mm(rows.reshape(-1, 2 * latents), dec1).astype(BF).reshape(half, -1, width)

    pieces_m = within(decode(wide[half:])).reshape(-1, width)
    sum_m = mm(flat(place_m), pieces_m, ROWS)
    sum_low_sent = sum_m.astype(BF)
    sum_low = across(sum_low_sent)
    pieces_o = within(decode(after(wide[:half], (sum_low_sent, received(0))))).reshape(-1, width)
    sum_o = mm(flat(place_o), pieces_o, ROWS) + decoder_bias[1] - mlp_target[1].astype(F32)
    sum_high_sent = sum_o.astype(BF)
    sum_high = across(sum_high_sent)

    error1 = ((sum_o + sum_low.astype(F32)) * scale).astype(BF)
    error1_m = ((sum_m + sum_high.astype(F32)) * scale).astype(BF)

    def send_errors(p, error):
        return within(mm(flat(p), error).astype(BF).reshape(half, layers * cap, width))

    error1 = after(error1, received(1))
    errors_o = send_errors(place_o, error1)

    errors_m = send_errors(place_m, after(error1_m, (errors_o, received(2))))
    residual1 = after(residual[1], (errors_m, received(3)))
    resid1 = everyone(mm(place[1], residual1).astype(BF).reshape(devices, cap, width))
    resid1 = resid1.reshape(slots, width)

    if direct:
        layer0 = jnp.stack(arrivals)
        pre0 = jnp.take(got_pre[:, 0], sender, axis=0).reshape(slots, latents)
    else:
        layer0 = arrivals[0]
        pre0 = got_pre[:, 0].reshape(slots, latents)
    target0 = layer0[:, :cap].reshape(slots, width)
    resid0 = layer0[:, cap:].reshape(slots, width)
    act0 = jnp.maximum(pre0, 0)
    piece00 = mm(act0, decoder[0]).astype(BF).astype(F32)
    error0 = ((piece00 + decoder_bias[0] - target0.astype(F32)) * scale).astype(BF)
    empty0 = (decoder_bias[0] * scale).astype(BF).astype(F32)
    empties = float(slots * devices - tokens * devices)

    def total(x):
        step = 1
        while step < devices:
            x = x + lax.ppermute(x, "layer", [(i, i ^ step) for i in range(devices)])
            step *= 2
        return x

    sums = total(
        jnp.stack([jnp.sum(error0.astype(F32), axis=0), jnp.sum(error1.astype(F32), axis=0)])
    )
    bias_grad = sums - jnp.stack([empties * empty0, jnp.zeros_like(empty0)])

    wide_o = wide[:half].reshape(-1, 2 * latents)
    wide_m = wide[half:].reshape(-1, 2 * latents)
    errors_o = errors_o.reshape(-1, width)
    errors_m = errors_m.reshape(-1, width)
    dec_later = mm(wide_o, errors_o, ROWS) + mm(wide_m, errors_m, ROWS)
    back = jnp.concatenate([mm(errors_o, dec1, LAST), mm(errors_m, dec1, LAST)], axis=0)
    back = back.reshape(devices, layers, cap, 2 * latents)
    back = turn(back)
    back0 = back[:, 0, :, :latents]
    if direct:
        back0 = jnp.take(back0, sender, axis=0)
    grad0 = back0.reshape(slots, latents) + mm(error0, decoder[0], LAST)
    grad0 = jnp.where(pre0 > 0, grad0, 0.0)
    grad1 = jnp.where(got_pre[:, 1] > 0, back[:, 1, :, latents:], 0.0).reshape(slots, latents)
    enc_bias = jnp.stack([jnp.sum(grad0, axis=0), jnp.sum(grad1, axis=0)])
    dec = jnp.concatenate(
        [mm(act0, error0, ROWS).astype(BF)[None], dec_later.astype(BF).reshape(2, latents, width)]
    )
    enc = jnp.stack(
        [
            mm(resid0, grad0.astype(BF), ROWS).astype(BF),
            mm(resid1, grad1.astype(BF), ROWS).astype(BF),
        ]
    )
    return dec, enc, enc_bias, bias_grad


def solution(mesh):
    return jax.shard_map(
        per_device,
        mesh=mesh,
        in_specs=(
            P(None, ("grp", "layer"), None),
            P(None, ("grp", "layer"), None),
            P(None, ("grp", "layer"), None, None),
            P(None, ("grp", "layer"), None),
            P(None, "layer", None),
            P(),
        ),
        out_specs=(
            P("grp", "layer", None),
            P("grp", None, "layer"),
            P("grp", "layer"),
            P("grp", None),
        ),
        check_vma=False,
    )
```

```python
import math

import jax
import jax.numpy as jnp
from jax import lax
from jax.experimental import pallas as pl
from jax.experimental.pallas import tpu as pltpu
from jax.sharding import PartitionSpec as P

BF = jnp.bfloat16
F32 = jnp.float32
ROWS = ((0,), (0,))
LAST = ((1,), (1,))


def mm(a, b, dims=((1,), (0,))):
    return lax.dot_general(a, b, (dims, ((), ())), preferred_element_type=F32)


def column_block(width):
    return next((b for b in (512, 256, 128) if width % b == 0), width)


def pack_rows(key, first, second, groups, cap):
    _, tokens, width = first.shape
    step = column_block(width)

    def kernel(key_ref, first_ref, second_ref, *outs):
        slot = lax.broadcasted_iota(jnp.int32, (groups * cap, tokens), 0)
        hot = (key_ref[...] == slot).astype(F32).astype(BF)
        for at, rows_ref in enumerate((first_ref, second_ref)):
            placed = mm(hot, rows_ref[0]).astype(BF)
            for k in range(groups):
                outs[k][at * cap : (at + 1) * cap, :] = placed[k * cap : (k + 1) * cap]

    rows_spec = pl.BlockSpec((1, tokens, step), lambda i: (0, 0, i))
    return pl.pallas_call(
        kernel,
        grid=(width // step,),
        in_specs=[pl.BlockSpec((1, tokens), lambda i: (0, 0)), rows_spec, rows_spec],
        out_specs=[pl.BlockSpec((2 * cap, step), lambda i: (0, i))] * groups,
        out_shape=[jax.ShapeDtypeStruct((2 * cap, width), BF)] * groups,
        compiler_params=pltpu.CompilerParams(vmem_limit_bytes=32 * 2**20),
        cost_estimate=pl.CostEstimate(
            flops=4 * groups * cap * tokens * width,
            bytes_accessed=4 * (tokens + groups * cap) * width,
            transcendentals=0,
        ),
    )(key, first, second)


def per_device(residual, mlp_target, pre_acts, blocks, decoder, decoder_bias):
    devices = lax.axis_size("layer")
    layers, tokens, width = residual.shape
    latents = pre_acts.shape[3]
    cap = max(2, 2 * tokens // devices)
    slots = devices * cap
    half = devices // 2
    scale = 1.0 / math.sqrt(tokens)
    me = lax.axis_index("layer")
    upper = me >= half
    mirror = [(i, (i + half) % devices) for i in range(devices)]
    halves = [list(range(half)), list(range(half, devices))]

    def everyone(x):
        return lax.all_to_all(x, "layer", split_axis=0, concat_axis=0, tiled=True)

    def within(x):
        return lax.all_to_all(
            x, "layer", split_axis=0, concat_axis=0, tiled=True, axis_index_groups=halves
        )

    def after(x, done):
        return lax.optimization_barrier((x, done))[0]

    def across(x):
        return lax.ppermute(x, "layer", mirror)

    def turn(x):
        first, second = x[: x.shape[0] // 2], x[x.shape[0] // 2 :]
        return jnp.concatenate(
            [jnp.where(upper, second, first), jnp.where(upper, first, second)], axis=0
        )

    routes = blocks.reshape(layers, tokens)
    earlier = jnp.arange(tokens)[:, None] > jnp.arange(tokens)[None, :]

    def ordinals(named):
        same = named[:, :, None] == named[:, None, :]
        return jnp.sum((same & earlier).astype(jnp.int32), axis=2)

    pre = pre_acts.reshape(layers, tokens, latents)

    order = ordinals(routes)
    routes_m, order_m = across(jnp.stack([routes, order]))
    slot_of = routes * cap + order
    place = (slot_of[:, None, :] == jnp.arange(slots, dtype=jnp.int32)[None, :, None]).astype(BF)

    def pair_places(named, order, base):
        block = base + jnp.arange(half, dtype=jnp.int32)[:, None, None, None]
        slot = jnp.arange(cap, dtype=jnp.int32)[None, None, :, None]
        hit = (named[None, :, None, :] == block) & (order[None, :, None, :] == slot)
        return hit.astype(BF).reshape(half, layers, cap, tokens)

    base = jnp.where(upper, half, 0).astype(jnp.int32)
    place_o = pair_places(routes, order, base)
    place_m = pair_places(routes_m, order_m, base)

    def flat(p):
        return p.reshape(-1, p.shape[-1])

    sent_pre = jnp.stack(
        [mm(place[l], pre[l]).astype(BF).reshape(devices, cap, latents) for l in range(layers)],
        axis=1,
    )
    got_pre = everyone(sent_pre.reshape(devices, layers * cap, latents))
    got_pre = got_pre.reshape(devices, layers, cap, latents)
    direct = devices <= 16 and cap % 16 == 0
    windows = [[8, 9, 10, 11, 12], [1, 2, 4], [3, 5], [6, 7, 13, 14, 15]]
    arrivals = [None] * devices
    if direct:
        windows = [[k for k in ks if k < devices] for ks in windows]
        key = ((routes[:1] ^ me) * cap + order[:1]).astype(jnp.int32)
        packed = pack_rows(key, mlp_target, residual, devices, cap)
        arrivals[0] = packed[0]
        sender = (me ^ jnp.arange(devices, dtype=jnp.int32)).astype(jnp.int32)

    def depart(window, begin):
        if not direct:
            return
        rows = [packed[k] for k in windows[window]]
        if begin is not None:
            rows = after(rows, begin)
        for k, x in zip(windows[window], rows):
            arrivals[k] = lax.ppermute(x, "layer", [(i, i ^ k) for i in range(devices)])

    def arrived(window):
        return [arrivals[k] for k in windows[window]] if direct else []

    acts = turn(jnp.maximum(got_pre, 0))
    nothing = jnp.zeros((devices, 1, cap, latents), BF)
    wide = jnp.concatenate(
        [
            jnp.concatenate([acts[:, 0:1], nothing], axis=3),
            jnp.concatenate([nothing, acts[:, 1:2]], axis=3),
        ],
        axis=1,
    ).reshape(devices, layers * cap, 2 * latents)
    dec1 = decoder[1:3].reshape(2 * latents, width)

    def decode(rows):
        return mm(rows.reshape(-1, 2 * latents), dec1).astype(BF).reshape(half, -1, width)

    depart(0, None)
    pieces_m = within(decode(wide[half:])).reshape(-1, width)
    sum_m = mm(flat(place_m), pieces_m, ROWS).astype(BF)
    sum_low = across(sum_m)
    depart(1, sum_m)
    pieces_o = decode(wide[:half])
    pieces_o = within(after(pieces_o, (sum_m, arrived(0)))).reshape(-1, width)
    sum_o = mm(flat(place_o), pieces_o, ROWS) + decoder_bias[1] - mlp_target[1].astype(F32)
    sum_o = sum_o.astype(BF)
    sum_high = across(sum_o)
    depart(2, sum_o)

    def add_halves(a, b):
        return ((a.astype(F32) + b.astype(F32)) * scale).astype(BF)

    def send_errors(p, error):
        return within(mm(flat(p), error).astype(BF).reshape(half, layers * cap, width))

    error1 = after(add_halves(sum_o, sum_low), arrived(1))
    errors_o = send_errors(place_o, error1)
    error1_m = after(add_halves(sum_m, sum_high), (errors_o, arrived(2)))
    depart(3, error1_m)
    errors_m = send_errors(place_m, error1_m)
    resid1 = mm(place[1], residual[1]).astype(BF).reshape(devices, cap, width)
    resid1 = everyone(after(resid1, (errors_m, arrived(3)))).reshape(slots, width)

    if direct:
        layer0 = jnp.stack(arrivals)
        pre0 = jnp.take(got_pre[:, 0], sender, axis=0).reshape(slots, latents)
    else:
        layer0 = everyone(
            jnp.concatenate(
                [
                    mm(place[0], rows[0]).astype(BF).reshape(devices, cap, width)
                    for rows in (mlp_target, residual)
                ],
                axis=1,
            )
        )
        pre0 = got_pre[:, 0].reshape(slots, latents)
    target0 = layer0[:, :cap].reshape(slots, width)
    resid0 = layer0[:, cap:].reshape(slots, width)
    act0 = jnp.maximum(pre0, 0)
    piece00 = mm(act0, decoder[0]).astype(BF).astype(F32)
    error0 = ((piece00 + decoder_bias[0] - target0.astype(F32)) * scale).astype(BF)
    empty0 = (decoder_bias[0] * scale).astype(BF).astype(F32)
    empties = float(slots * devices - tokens * devices)

    def total(x):
        step = devices // 2
        while step >= 1:
            x = x + lax.ppermute(x, "layer", [(i, i ^ step) for i in range(devices)])
            step //= 2
        return x

    sums = total(
        jnp.stack([jnp.sum(error0.astype(F32), axis=0), jnp.sum(error1.astype(F32), axis=0)])
    )
    bias_grad = sums - jnp.stack([empties * empty0, jnp.zeros_like(empty0)])

    wide_o = wide[:half].reshape(-1, 2 * latents)
    wide_m = wide[half:].reshape(-1, 2 * latents)
    errors_o = errors_o.reshape(-1, width)
    errors_m = errors_m.reshape(-1, width)
    dec_later = mm(wide_o, errors_o, ROWS) + mm(wide_m, errors_m, ROWS)
    back = jnp.concatenate([mm(errors_o, dec1, LAST), mm(errors_m, dec1, LAST)], axis=0)
    back = back.reshape(devices, layers, cap, 2 * latents)
    back = turn(back)
    back0 = back[:, 0, :, :latents]
    if direct:
        back0 = jnp.take(back0, sender, axis=0)
    grad0 = back0.reshape(slots, latents) + mm(error0, decoder[0], LAST)
    grad0 = jnp.where(pre0 > 0, grad0, 0.0)
    grad1 = jnp.where(got_pre[:, 1] > 0, back[:, 1, :, latents:], 0.0).reshape(slots, latents)
    enc_bias = jnp.stack([jnp.sum(grad0, axis=0), jnp.sum(grad1, axis=0)])
    dec = jnp.concatenate(
        [mm(act0, error0, ROWS).astype(BF)[None], dec_later.astype(BF).reshape(2, latents, width)]
    )
    enc = jnp.stack(
        [
            mm(resid0, grad0.astype(BF), ROWS).astype(BF),
            mm(resid1, grad1.astype(BF), ROWS).astype(BF),
        ]
    )
    return dec, enc, enc_bias, bias_grad


def solution(mesh):
    return jax.shard_map(
        per_device,
        mesh=mesh,
        in_specs=(
            P(None, ("grp", "layer"), None),
            P(None, ("grp", "layer"), None),
            P(None, ("grp", "layer"), None, None),
            P(None, ("grp", "layer"), None),
            P(None, "layer", None),
            P(),
        ),
        out_specs=(
            P("grp", "layer", None),
            P("grp", None, "layer"),
            P("grp", "layer"),
            P("grp", None),
        ),
        check_vma=False,
    )
```

```python
import math

import jax
import jax.numpy as jnp
from jax import lax
from jax.experimental import pallas as pl
from jax.experimental.pallas import tpu as pltpu
from jax.sharding import PartitionSpec as P

BF = jnp.bfloat16
F32 = jnp.float32
ROWS = ((0,), (0,))
LAST = ((1,), (1,))


def mm(a, b, dims=((1,), (0,))):
    return lax.dot_general(a, b, (dims, ((), ())), preferred_element_type=F32)


def column_block(width):
    return next((b for b in (512, 256, 128) if width % b == 0), width)


def pack_rows(key, first, second, groups, cap):
    _, tokens, width = first.shape
    step = column_block(width)

    def kernel(key_ref, first_ref, second_ref, *outs):
        slot = lax.broadcasted_iota(jnp.int32, (groups * cap, tokens), 0)
        hot = (key_ref[...] == slot).astype(F32).astype(BF)
        for at, rows_ref in enumerate((first_ref, second_ref)):
            placed = mm(hot, rows_ref[0]).astype(BF)
            for k in range(groups):
                outs[k][at * cap : (at + 1) * cap, :] = placed[k * cap : (k + 1) * cap]

    rows_spec = pl.BlockSpec((1, tokens, step), lambda i: (0, 0, i))
    return pl.pallas_call(
        kernel,
        grid=(width // step,),
        in_specs=[pl.BlockSpec((1, tokens), lambda i: (0, 0)), rows_spec, rows_spec],
        out_specs=[pl.BlockSpec((2 * cap, step), lambda i: (0, i))] * groups,
        out_shape=[jax.ShapeDtypeStruct((2 * cap, width), BF)] * groups,
        compiler_params=pltpu.CompilerParams(vmem_limit_bytes=32 * 2**20),
        cost_estimate=pl.CostEstimate(
            flops=4 * groups * cap * tokens * width,
            bytes_accessed=4 * (tokens + groups * cap) * width,
            transcendentals=0,
        ),
    )(key, first, second)


def layer0_errors(arrivals, act, decoder, bias, scale, cap):
    groups = len(arrivals)
    slots, latents = act.shape
    layers, width = bias.shape
    step = column_block(width)

    def kernel(act_ref, dec_ref, bias_ref, *refs):
        rows = refs[:groups]
        sum_ref, grad_ref, back_ref, target = refs[groups:]
        for k in range(groups):
            target[k * cap : (k + 1) * cap, :] = rows[k][:cap, :]
        piece = mm(act_ref[...], dec_ref[0]).astype(BF).astype(F32)
        error = (piece + bias_ref[0:1, :] - target[...].astype(F32)) * scale
        error = error.astype(BF)
        sum_ref[...] = jnp.sum(error.astype(F32), axis=0, keepdims=True)
        grad_ref[...] = mm(act_ref[...], error, ROWS).astype(BF)

        @pl.when(pl.program_id(0) == 0)
        def _():
            back_ref[...] = jnp.zeros_like(back_ref)

        back_ref[...] += mm(error, dec_ref[0], LAST)

    return pl.pallas_call(
        kernel,
        grid=(width // step,),
        in_specs=[
            pl.BlockSpec((slots, latents), lambda i: (0, 0)),
            pl.BlockSpec((1, latents, step), lambda i: (0, 0, i)),
            pl.BlockSpec((layers, step), lambda i: (0, i)),
        ]
        + [pl.BlockSpec((2 * cap, step), lambda i: (0, i))] * groups,
        out_specs=[
            pl.BlockSpec((1, step), lambda i: (0, i)),
            pl.BlockSpec((latents, step), lambda i: (0, i)),
            pl.BlockSpec((slots, latents), lambda i: (0, 0)),
        ],
        out_shape=[
            jax.ShapeDtypeStruct((1, width), F32),
            jax.ShapeDtypeStruct((latents, width), BF),
            jax.ShapeDtypeStruct((slots, latents), F32),
        ],
        scratch_shapes=[pltpu.VMEM((slots, step), BF)],
        compiler_params=pltpu.CompilerParams(vmem_limit_bytes=32 * 2**20),
        cost_estimate=pl.CostEstimate(
            flops=6 * slots * latents * width,
            bytes_accessed=2 * (2 * slots + 2 * latents) * width,
            transcendentals=0,
        ),
    )(act, decoder, bias, *arrivals)


def encoder_layer0(arrivals, low, layers, cap):
    groups = len(arrivals)
    slots, latents = low.shape
    width = arrivals[0].shape[1]
    step = column_block(width)

    def kernel(low_ref, *refs):
        rows, out_ref, resid = refs[:groups], refs[groups], refs[groups + 1]
        for k in range(groups):
            resid[k * cap : (k + 1) * cap, :] = rows[k][cap:, :]
        out_ref[0] = mm(resid[...], low_ref[...], ROWS).astype(BF)

    return pl.pallas_call(
        kernel,
        grid=(width // step,),
        in_specs=[pl.BlockSpec((slots, latents), lambda i: (0, 0))]
        + [pl.BlockSpec((2 * cap, step), lambda i: (0, i))] * groups,
        out_specs=pl.BlockSpec((1, step, latents), lambda i: (0, i, 0)),
        out_shape=jax.ShapeDtypeStruct((layers, width, latents), BF),
        scratch_shapes=[pltpu.VMEM((slots, step), BF)],
        compiler_params=pltpu.CompilerParams(vmem_limit_bytes=32 * 2**20),
        cost_estimate=pl.CostEstimate(
            flops=2 * slots * latents * width,
            bytes_accessed=2 * (2 * slots + latents) * width,
            transcendentals=0,
        ),
    )(low, *arrivals)


def encoder_layer1(products, resid, low):
    slots, latents = low.shape
    width = resid.shape[1]
    step = column_block(width)

    def kernel(low_ref, resid_ref, _, out_ref):
        out_ref[0] = mm(resid_ref[...], low_ref[...], ROWS).astype(BF)

    return pl.pallas_call(
        kernel,
        grid=(width // step,),
        in_specs=[
            pl.BlockSpec((slots, latents), lambda i: (0, 0)),
            pl.BlockSpec((slots, step), lambda i: (0, i)),
            pl.BlockSpec(memory_space=pl.ANY),
        ],
        out_specs=pl.BlockSpec((1, step, latents), lambda i: (1, i, 0)),
        out_shape=jax.ShapeDtypeStruct(products.shape, BF),
        input_output_aliases={2: 0},
        compiler_params=pltpu.CompilerParams(vmem_limit_bytes=32 * 2**20),
        cost_estimate=pl.CostEstimate(
            flops=2 * slots * latents * width,
            bytes_accessed=2 * (slots + latents) * width,
            transcendentals=0,
        ),
    )(low, resid, products)


def per_device(residual, mlp_target, pre_acts, blocks, decoder, decoder_bias):
    devices = lax.axis_size("layer")
    layers, tokens, width = residual.shape
    latents = pre_acts.shape[3]
    cap = max(2, 2 * tokens // devices)
    slots = devices * cap
    half = devices // 2
    scale = 1.0 / math.sqrt(tokens)
    me = lax.axis_index("layer")
    upper = me >= half
    mirror = [(i, (i + half) % devices) for i in range(devices)]
    halves = [list(range(half)), list(range(half, devices))]

    def everyone(x):
        return lax.all_to_all(x, "layer", split_axis=0, concat_axis=0, tiled=True)

    def within(x):
        return lax.all_to_all(
            x, "layer", split_axis=0, concat_axis=0, tiled=True, axis_index_groups=halves
        )

    def after(x, done):
        return lax.optimization_barrier((x, done))[0]

    def across(x):
        return lax.ppermute(x, "layer", mirror)

    def turn(x):
        first, second = x[: x.shape[0] // 2], x[x.shape[0] // 2 :]
        return jnp.concatenate(
            [jnp.where(upper, second, first), jnp.where(upper, first, second)], axis=0
        )

    routes = blocks.reshape(layers, tokens)
    earlier = jnp.arange(tokens)[:, None] > jnp.arange(tokens)[None, :]

    def ordinals(named):
        same = named[:, :, None] == named[:, None, :]
        return jnp.sum((same & earlier).astype(jnp.int32), axis=2)

    pre = pre_acts.reshape(layers, tokens, latents)

    order = ordinals(routes)
    routes_m, order_m = across(jnp.stack([routes, order]))
    slot_of = routes * cap + order
    place = (slot_of[:, None, :] == jnp.arange(slots, dtype=jnp.int32)[None, :, None]).astype(BF)

    def pair_places(named, order, base):
        block = base + jnp.arange(half, dtype=jnp.int32)[:, None, None, None]
        slot = jnp.arange(cap, dtype=jnp.int32)[None, None, :, None]
        hit = (named[None, :, None, :] == block) & (order[None, :, None, :] == slot)
        return hit.astype(BF).reshape(half, layers, cap, tokens)

    base = jnp.where(upper, half, 0).astype(jnp.int32)
    place_o = pair_places(routes, order, base)
    place_m = pair_places(routes_m, order_m, base)

    def flat(p):
        return p.reshape(-1, p.shape[-1])

    sent_pre = jnp.stack(
        [mm(place[l], pre[l]).astype(BF).reshape(devices, cap, latents) for l in range(layers)],
        axis=1,
    )
    got_pre = everyone(sent_pre.reshape(devices, layers * cap, latents))
    got_pre = got_pre.reshape(devices, layers, cap, latents)
    direct = devices <= 16 and cap % 16 == 0
    windows = [[10, 11, 12], [1, 2, 4], [3, 5], [6, 7, 13, 14, 15], [8, 9]]
    arrivals = [None] * devices
    if direct:
        windows = [[k for k in ks if k < devices] for ks in windows]
        key = ((routes[:1] ^ me) * cap + order[:1]).astype(jnp.int32)
        packed = pack_rows(key, mlp_target, residual, devices, cap)
        arrivals[0] = packed[0]
        sender = (me ^ jnp.arange(devices, dtype=jnp.int32)).astype(jnp.int32)

    def depart(window, begin):
        if not direct:
            return
        rows = [packed[k] for k in windows[window]]
        if begin is not None:
            rows = after(rows, begin)
        for k, x in zip(windows[window], rows):
            arrivals[k] = lax.ppermute(x, "layer", [(i, i ^ k) for i in range(devices)])

    def arrived(window):
        return [arrivals[k] for k in windows[window]] if direct else []

    acts = turn(jnp.maximum(got_pre, 0))
    nothing = jnp.zeros((devices, 1, cap, latents), BF)
    wide = jnp.concatenate(
        [
            jnp.concatenate([acts[:, 0:1], nothing], axis=3),
            jnp.concatenate([nothing, acts[:, 1:2]], axis=3),
        ],
        axis=1,
    ).reshape(devices, layers * cap, 2 * latents)
    dec1 = decoder[1:3].reshape(2 * latents, width)

    def decode(rows):
        return mm(rows.reshape(-1, 2 * latents), dec1).astype(BF).reshape(half, -1, width)

    depart(4, None)
    depart(0, None)
    pieces_m = decode(wide[half:])
    pieces_m = within(after(pieces_m, arrived(4))).reshape(-1, width)
    sum_m = mm(flat(place_m), pieces_m, ROWS).astype(BF)
    sum_low = across(sum_m)
    depart(1, sum_m)
    pieces_o = decode(wide[:half])
    if direct:
        pre0 = jnp.take(got_pre[:, 0], sender, axis=0).reshape(slots, latents)
    else:
        pre0 = got_pre[:, 0].reshape(slots, latents)
    act0 = jnp.maximum(pre0, 0)
    pieces_o = within(after(pieces_o, (sum_m, act0, arrived(0)))).reshape(-1, width)
    sum_o = mm(flat(place_o), pieces_o, ROWS) + decoder_bias[1] - mlp_target[1].astype(F32)
    sum_o = sum_o.astype(BF)
    sum_high = across(sum_o)
    depart(2, sum_o)

    def add_halves(a, b):
        return ((a.astype(F32) + b.astype(F32)) * scale).astype(BF)

    def send_errors(p, error):
        return within(mm(flat(p), error).astype(BF).reshape(half, layers * cap, width))

    error1 = after(add_halves(sum_o, sum_low), arrived(1))
    errors_o = send_errors(place_o, error1)
    error1_m = after(add_halves(sum_m, sum_high), (errors_o, arrived(2)))
    depart(3, error1_m)
    errors_m = send_errors(place_m, error1_m)
    resid1 = mm(place[1], residual[1]).astype(BF).reshape(devices, cap, width)
    resid1 = everyone(after(resid1, (errors_m, arrived(3)))).reshape(slots, width)

    empty0 = (decoder_bias[0] * scale).astype(BF).astype(F32)
    empties = float(slots * devices - tokens * devices)
    if direct:
        sum0, dec0, own = layer0_errors(arrivals, act0, decoder, decoder_bias, scale, cap)
    else:
        layer0 = everyone(
            jnp.concatenate(
                [
                    mm(place[0], rows[0]).astype(BF).reshape(devices, cap, width)
                    for rows in (mlp_target, residual)
                ],
                axis=1,
            )
        )
        target0 = layer0[:, :cap].reshape(slots, width)
        resid0 = layer0[:, cap:].reshape(slots, width)
        piece00 = mm(act0, decoder[0]).astype(BF).astype(F32)
        error0 = ((piece00 + decoder_bias[0] - target0.astype(F32)) * scale).astype(BF)
        sum0 = jnp.sum(error0.astype(F32), axis=0, keepdims=True)
        dec0 = mm(act0, error0, ROWS).astype(BF)
        own = mm(error0, decoder[0], LAST)

    def total(x):
        step = devices // 2
        while step >= 1:
            x = x + lax.ppermute(x, "layer", [(i, i ^ step) for i in range(devices)])
            step //= 2
        return x

    sums = total(
        jnp.concatenate([sum0, jnp.sum(error1.astype(F32), axis=0, keepdims=True)])
    )
    bias_grad = sums - jnp.stack([empties * empty0, jnp.zeros_like(empty0)])

    wide_o = wide[:half].reshape(-1, 2 * latents)
    wide_m = wide[half:].reshape(-1, 2 * latents)
    errors_o = errors_o.reshape(-1, width)
    errors_m = errors_m.reshape(-1, width)
    dec_later = mm(wide_o, errors_o, ROWS) + mm(wide_m, errors_m, ROWS)
    back = jnp.concatenate([mm(errors_o, dec1, LAST), mm(errors_m, dec1, LAST)], axis=0)
    back = back.reshape(devices, layers, cap, 2 * latents)
    back = turn(back)
    back0 = back[:, 0, :, :latents]
    if direct:
        back0 = jnp.take(back0, sender, axis=0)
    grad0 = back0.reshape(slots, latents) + own
    grad0 = jnp.where(pre0 > 0, grad0, 0.0)
    grad1 = jnp.where(got_pre[:, 1] > 0, back[:, 1, :, latents:], 0.0).reshape(slots, latents)
    enc_bias = jnp.stack([jnp.sum(grad0, axis=0), jnp.sum(grad1, axis=0)])
    dec = jnp.concatenate([dec0[None], dec_later.astype(BF).reshape(2, latents, width)])
    low0, low1 = grad0.astype(BF), grad1.astype(BF)
    if direct:
        enc = encoder_layer1(encoder_layer0(arrivals, low0, layers, cap), resid1, low1)
    else:
        enc = jnp.stack([mm(resid0, low0, ROWS).astype(BF), mm(resid1, low1, ROWS).astype(BF)])
    return dec, enc, enc_bias, bias_grad


def solution(mesh):
    return jax.shard_map(
        per_device,
        mesh=mesh,
        in_specs=(
            P(None, ("grp", "layer"), None),
            P(None, ("grp", "layer"), None),
            P(None, ("grp", "layer"), None, None),
            P(None, ("grp", "layer"), None),
            P(None, "layer", None),
            P(),
        ),
        out_specs=(
            P("grp", "layer", None),
            P("grp", None, "layer"),
            P("grp", "layer"),
            P("grp", None),
        ),
        check_vma=False,
    )
```

```python
import math

import jax
import jax.numpy as jnp
from jax import lax
from jax.experimental import pallas as pl
from jax.experimental.pallas import tpu as pltpu
from jax.sharding import PartitionSpec as P

BF = jnp.bfloat16
F32 = jnp.float32
ROWS = ((0,), (0,))
LAST = ((1,), (1,))
SMALL = pl.CostEstimate(flops=1, bytes_accessed=1, transcendentals=0)
PARAMS = pltpu.CompilerParams(vmem_limit_bytes=56 * 2**20)


def mm(a, b, dims=((1,), (0,))):
    return lax.dot_general(a, b, (dims, ((), ())), preferred_element_type=F32)


def column_block(width):
    return next((b for b in (512, 256, 128) if width % b == 0), width)


def pack_rows(key, first, second, groups, cap):
    _, tokens, width = first.shape
    step = column_block(width)

    def kernel(key_ref, first_ref, second_ref, *outs):
        slot = lax.broadcasted_iota(jnp.int32, (groups * cap, tokens), 0)
        hot = (key_ref[...] == slot).astype(F32).astype(BF)
        for at, rows_ref in enumerate((first_ref, second_ref)):
            placed = mm(hot, rows_ref[0]).astype(BF)
            for k in range(groups):
                outs[k][at * cap : (at + 1) * cap, :] = placed[k * cap : (k + 1) * cap]

    rows_spec = pl.BlockSpec((1, tokens, step), lambda i: (0, 0, i))
    return pl.pallas_call(
        kernel,
        grid=(width // step,),
        in_specs=[pl.BlockSpec((1, tokens), lambda i: (0, 0)), rows_spec, rows_spec],
        out_specs=[pl.BlockSpec((2 * cap, step), lambda i: (0, i))] * groups,
        out_shape=[jax.ShapeDtypeStruct((2 * cap, width), BF)] * groups,
        compiler_params=PARAMS,
        cost_estimate=SMALL,
    )(key, first, second)


def layer0_errors(arrivals, act, decoder, bias, scale, cap):
    groups = len(arrivals)
    slots, latents = act.shape
    layers, width = bias.shape
    step = column_block(width)

    def kernel(act_ref, dec_ref, bias_ref, *refs):
        rows = refs[:groups]
        sum_ref, grad_ref, back_ref, target = refs[groups:]
        for k in range(groups):
            target[k * cap : (k + 1) * cap, :] = rows[k][:cap, :]
        piece = mm(act_ref[...], dec_ref[0]).astype(BF).astype(F32)
        error = (piece + bias_ref[0:1, :] - target[...].astype(F32)) * scale
        error = error.astype(BF)
        sum_ref[...] = jnp.sum(error.astype(F32), axis=0, keepdims=True)
        grad_ref[...] = mm(act_ref[...], error, ROWS).astype(BF)

        @pl.when(pl.program_id(0) == 0)
        def _():
            back_ref[...] = jnp.zeros_like(back_ref)

        back_ref[...] += mm(error, dec_ref[0], LAST)

    return pl.pallas_call(
        kernel,
        grid=(width // step,),
        in_specs=[
            pl.BlockSpec((slots, latents), lambda i: (0, 0)),
            pl.BlockSpec((1, latents, step), lambda i: (0, 0, i)),
            pl.BlockSpec((layers, step), lambda i: (0, i)),
        ]
        + [pl.BlockSpec((2 * cap, step), lambda i: (0, i))] * groups,
        out_specs=[
            pl.BlockSpec((1, step), lambda i: (0, i)),
            pl.BlockSpec((latents, step), lambda i: (0, i)),
            pl.BlockSpec((slots, latents), lambda i: (0, 0)),
        ],
        out_shape=[
            jax.ShapeDtypeStruct((1, width), F32),
            jax.ShapeDtypeStruct((latents, width), BF),
            jax.ShapeDtypeStruct((slots, latents), F32),
        ],
        scratch_shapes=[pltpu.VMEM((slots, step), BF)],
        compiler_params=PARAMS,
        cost_estimate=SMALL,
    )(act, decoder, bias, *arrivals)


def encoder_layer0(arrivals, low, layers, cap):
    groups = len(arrivals)
    slots, latents = low.shape
    width = arrivals[0].shape[1]
    step = column_block(width)

    def kernel(low_ref, *refs):
        rows, out_ref, resid = refs[:groups], refs[groups], refs[groups + 1]
        for k in range(groups):
            resid[k * cap : (k + 1) * cap, :] = rows[k][cap:, :]
        out_ref[0] = mm(resid[...], low_ref[...], ROWS).astype(BF)

    return pl.pallas_call(
        kernel,
        grid=(width // step,),
        in_specs=[pl.BlockSpec((slots, latents), lambda i: (0, 0))]
        + [pl.BlockSpec((2 * cap, step), lambda i: (0, i))] * groups,
        out_specs=pl.BlockSpec((1, step, latents), lambda i: (0, i, 0)),
        out_shape=jax.ShapeDtypeStruct((layers, width, latents), BF),
        scratch_shapes=[pltpu.VMEM((slots, step), BF)],
        compiler_params=PARAMS,
        cost_estimate=SMALL,
    )(low, *arrivals)


def encoder_layer1(products, resid, low):
    slots, latents = low.shape
    width = resid.shape[1]
    step = column_block(width)

    def kernel(low_ref, resid_ref, _, out_ref):
        out_ref[0] = mm(resid_ref[...], low_ref[...], ROWS).astype(BF)

    return pl.pallas_call(
        kernel,
        grid=(width // step,),
        in_specs=[
            pl.BlockSpec((slots, latents), lambda i: (0, 0)),
            pl.BlockSpec((slots, step), lambda i: (0, i)),
            pl.BlockSpec(memory_space=pl.ANY),
        ],
        out_specs=pl.BlockSpec((1, step, latents), lambda i: (1, i, 0)),
        out_shape=jax.ShapeDtypeStruct(products.shape, BF),
        input_output_aliases={2: 0},
        compiler_params=PARAMS,
        cost_estimate=SMALL,
    )(low, resid, products)


def gradients(me, errors, wide, decoder, pres, own, dec0, cap):
    devices = pres.shape[0]
    half = devices // 2
    pairs, latents, width = decoder.shape
    slots = devices * cap
    step = column_block(width)
    steps = width // step

    def kernel(me_ref, eo_ref, em_ref, wo_ref, wm_ref, dec1_ref, dec2_ref, pre_ref, own_ref, dec0_ref, dec_ref, low_ref, bias_ref, back):
        at = pl.program_id(0)
        grad = mm(wo_ref[...], eo_ref[...], ROWS) + mm(wm_ref[...], em_ref[...], ROWS)
        dec_ref[0] = dec0_ref[...]
        dec_ref[1] = grad[:latents].astype(BF)
        dec_ref[2] = grad[latents:].astype(BF)

        @pl.when(at == 0)
        def _():
            back[...] = jnp.zeros_like(back)

        both = jnp.concatenate([dec1_ref[0], dec2_ref[0]], axis=0)
        back[0] += mm(eo_ref[...], both, LAST)
        back[1] += mm(em_ref[...], both, LAST)

        @pl.when(at == steps - 1)
        def _():
            my = me_ref[0]
            sums = [jnp.zeros((1, latents), F32) for _ in range(2)]
            for k in range(devices):
                group = (my ^ k) % half
                sender = my ^ k
                for l in range(2):
                    at_row = pl.multiple_of(group * 2 * cap + l * cap, cap)
                    part = back[k // half, pl.ds(at_row, cap), l * latents : (l + 1) * latents]
                    if l == 0:
                        part = part + own_ref[k * cap : (k + 1) * cap, :]
                        place = k * cap
                    else:
                        place = pl.multiple_of(sender * cap, cap)
                    pre = pre_ref[(k // half) * half + group, l * cap : (l + 1) * cap, :]
                    part = jnp.where(pre.astype(F32) > 0, part, 0.0)
                    sums[l] = sums[l] + jnp.sum(part, axis=0, keepdims=True)
                    low_ref[l, pl.ds(place, cap), :] = part.astype(BF)
            for l in range(2):
                bias_ref[l : l + 1, :] = sums[l]

    whole = lambda shape: pl.BlockSpec(shape, lambda i: (0,) * len(shape))
    return pl.pallas_call(
        kernel,
        grid=(steps,),
        in_specs=[pl.BlockSpec(memory_space=pltpu.SMEM)]
        + [pl.BlockSpec((half * 2 * cap, step), lambda i: (0, i))] * 2
        + [whole((half * 2 * cap, 2 * latents))] * 2
        + [
            pl.BlockSpec((1, latents, step), lambda i: (1, 0, i)),
            pl.BlockSpec((1, latents, step), lambda i: (2, 0, i)),
            whole((devices, 2 * cap, latents)),
            whole((slots, latents)),
            pl.BlockSpec((latents, step), lambda i: (0, i)),
        ],
        out_specs=[
            pl.BlockSpec((pairs, latents, step), lambda i: (0, 0, i)),
            whole((2, slots, latents)),
            whole((2, latents)),
        ],
        out_shape=[
            jax.ShapeDtypeStruct((pairs, latents, width), BF),
            jax.ShapeDtypeStruct((2, slots, latents), BF),
            jax.ShapeDtypeStruct((2, latents), F32),
        ],
        scratch_shapes=[pltpu.VMEM((2, half * 2 * cap, 2 * latents), F32)],
        compiler_params=PARAMS,
        cost_estimate=SMALL,
    )(me, *errors, *wide, decoder, decoder, pres, own, dec0)


def per_device(residual, mlp_target, pre_acts, blocks, decoder, decoder_bias):
    devices = lax.axis_size("layer")
    layers, tokens, width = residual.shape
    latents = pre_acts.shape[3]
    cap = max(2, 2 * tokens // devices)
    slots = devices * cap
    half = devices // 2
    scale = 1.0 / math.sqrt(tokens)
    me = lax.axis_index("layer")
    upper = me >= half
    mirror = [(i, (i + half) % devices) for i in range(devices)]
    halves = [list(range(half)), list(range(half, devices))]

    def everyone(x):
        return lax.all_to_all(x, "layer", split_axis=0, concat_axis=0, tiled=True)

    def within(x):
        return lax.all_to_all(
            x, "layer", split_axis=0, concat_axis=0, tiled=True, axis_index_groups=halves
        )

    def after(x, done):
        return lax.optimization_barrier((x, done))[0]

    def across(x):
        return lax.ppermute(x, "layer", mirror)

    def turn(x):
        first, second = x[: x.shape[0] // 2], x[x.shape[0] // 2 :]
        return jnp.concatenate(
            [jnp.where(upper, second, first), jnp.where(upper, first, second)], axis=0
        )

    routes = blocks.reshape(layers, tokens)
    earlier = jnp.arange(tokens)[:, None] > jnp.arange(tokens)[None, :]

    def ordinals(named):
        same = named[:, :, None] == named[:, None, :]
        return jnp.sum((same & earlier).astype(jnp.int32), axis=2)

    pre = pre_acts.reshape(layers, tokens, latents)

    order = ordinals(routes)
    routes_m, order_m = across(jnp.stack([routes, order]))
    slot_of = routes * cap + order
    place = (slot_of[:, None, :] == jnp.arange(slots, dtype=jnp.int32)[None, :, None]).astype(BF)

    def pair_places(named, order, base):
        block = base + jnp.arange(half, dtype=jnp.int32)[:, None, None, None]
        slot = jnp.arange(cap, dtype=jnp.int32)[None, None, :, None]
        hit = (named[None, :, None, :] == block) & (order[None, :, None, :] == slot)
        return hit.astype(BF).reshape(half, layers, cap, tokens)

    base = jnp.where(upper, half, 0).astype(jnp.int32)
    place_o = pair_places(routes, order, base)
    place_m = pair_places(routes_m, order_m, base)

    def flat(p):
        return p.reshape(-1, p.shape[-1])

    sent_pre = jnp.stack(
        [mm(place[l], pre[l]).astype(BF).reshape(devices, cap, latents) for l in range(layers)],
        axis=1,
    )
    got_pre = everyone(sent_pre.reshape(devices, layers * cap, latents))
    got_pre = got_pre.reshape(devices, layers, cap, latents)
    direct = devices <= 16 and cap % 16 == 0
    windows = [[8, 9, 10], [1, 2, 4], [3, 5], [6, 7, 11, 12, 13, 14, 15]]
    arrivals = [None] * devices
    if direct:
        windows = [[k for k in ks if k < devices] for ks in windows]
        key = ((routes[:1] ^ me) * cap + order[:1]).astype(jnp.int32)
        packed = pack_rows(key, mlp_target, residual, devices, cap)
        arrivals[0] = packed[0]
        sender = (me ^ jnp.arange(devices, dtype=jnp.int32)).astype(jnp.int32)

    def depart(window, begin):
        if not direct:
            return
        rows = [packed[k] for k in windows[window]]
        if begin is not None:
            rows = after(rows, begin)
        for k, x in zip(windows[window], rows):
            arrivals[k] = lax.ppermute(x, "layer", [(i, i ^ k) for i in range(devices)])

    def arrived(window):
        return [arrivals[k] for k in windows[window]] if direct else []

    acts = turn(jnp.maximum(got_pre, 0))
    nothing = jnp.zeros((devices, 1, cap, latents), BF)
    wide = jnp.concatenate(
        [
            jnp.concatenate([acts[:, 0:1], nothing], axis=3),
            jnp.concatenate([nothing, acts[:, 1:2]], axis=3),
        ],
        axis=1,
    ).reshape(devices, layers * cap, 2 * latents)
    dec1 = decoder[1:3].reshape(2 * latents, width)

    def decode(rows):
        return mm(rows.reshape(-1, 2 * latents), dec1).astype(BF).reshape(half, -1, width)

    depart(0, None)
    pieces_m = decode(wide[half:])
    pieces_m = after(pieces_m, packed) if direct else pieces_m
    pieces_m = within(pieces_m).reshape(-1, width)
    sum_m = mm(flat(place_m), pieces_m, ROWS).astype(BF)
    sum_low = across(sum_m)
    depart(1, sum_m)
    pieces_o = decode(wide[:half])
    if direct:
        pre0 = jnp.take(got_pre[:, 0], sender, axis=0).reshape(slots, latents)
    else:
        pre0 = got_pre[:, 0].reshape(slots, latents)
    act0 = jnp.maximum(pre0, 0)
    pieces_o = within(after(pieces_o, (sum_m, act0, arrived(0)))).reshape(-1, width)
    sum_o = mm(flat(place_o), pieces_o, ROWS) + decoder_bias[1] - mlp_target[1].astype(F32)
    sum_o = sum_o.astype(BF)
    sum_high = across(sum_o)
    depart(2, sum_o)

    def add_halves(a, b):
        return ((a.astype(F32) + b.astype(F32)) * scale).astype(BF)

    def send_errors(p, error):
        return within(mm(flat(p), error).astype(BF).reshape(half, layers * cap, width))

    error1 = after(add_halves(sum_o, sum_low), arrived(1))
    errors_o = send_errors(place_o, error1)
    error1_m = after(add_halves(sum_m, sum_high), (errors_o, arrived(2)))
    depart(3, error1_m)
    errors_m = send_errors(place_m, error1_m)
    resid1 = mm(place[1], residual[1]).astype(BF).reshape(devices, cap, width)
    resid1 = everyone(after(resid1, (errors_m, arrived(3)))).reshape(slots, width)

    empty0 = (decoder_bias[0] * scale).astype(BF).astype(F32)
    empties = float(slots * devices - tokens * devices)
    if direct:
        sum0, dec0, own = layer0_errors(arrivals, act0, decoder, decoder_bias, scale, cap)
    else:
        layer0 = everyone(
            jnp.concatenate(
                [
                    mm(place[0], rows[0]).astype(BF).reshape(devices, cap, width)
                    for rows in (mlp_target, residual)
                ],
                axis=1,
            )
        )
        target0 = layer0[:, :cap].reshape(slots, width)
        resid0 = layer0[:, cap:].reshape(slots, width)
        piece00 = mm(act0, decoder[0]).astype(BF).astype(F32)
        error0 = ((piece00 + decoder_bias[0] - target0.astype(F32)) * scale).astype(BF)
        sum0 = jnp.sum(error0.astype(F32), axis=0, keepdims=True)
        dec0 = mm(act0, error0, ROWS).astype(BF)
        own = mm(error0, decoder[0], LAST)

    def total(x):
        step = devices // 2
        while step >= 1:
            x = x + lax.ppermute(x, "layer", [(i, i ^ step) for i in range(devices)])
            step //= 2
        return x

    sums = total(
        jnp.concatenate([sum0, jnp.sum(error1.astype(F32), axis=0, keepdims=True)])
    )
    bias_grad = sums - jnp.stack([empties * empty0, jnp.zeros_like(empty0)])

    wide_o = wide[:half].reshape(-1, 2 * latents)
    wide_m = wide[half:].reshape(-1, 2 * latents)
    errors_o = errors_o.reshape(-1, width)
    errors_m = errors_m.reshape(-1, width)
    if direct:
        pres = turn(got_pre).reshape(devices, layers * cap, latents)
        dec, low, enc_bias = gradients(
            me.astype(jnp.int32).reshape(1),
            (errors_o, errors_m),
            (wide_o, wide_m),
            decoder,
            pres,
            own,
            dec0,
            cap,
        )
        enc = encoder_layer1(encoder_layer0(arrivals, low[0], layers, cap), resid1, low[1])
    else:
        dec_later = mm(wide_o, errors_o, ROWS) + mm(wide_m, errors_m, ROWS)
        dec = jnp.concatenate([dec0[None], dec_later.astype(BF).reshape(2, latents, width)])
        back = jnp.concatenate([mm(errors_o, dec1, LAST), mm(errors_m, dec1, LAST)], axis=0)
        back = turn(back.reshape(devices, layers, cap, 2 * latents))
        own = own.reshape(devices, cap, latents)
        grads = jnp.stack([back[:, 0, :, :latents] + own, back[:, 1, :, latents:]])
        grads = jnp.where(jnp.swapaxes(got_pre, 0, 1) > 0, grads, 0.0)
        grads = grads.reshape(layers, slots, latents)
        enc_bias = jnp.sum(grads, axis=1)
        low = grads.astype(BF)
        enc = jnp.stack([mm(resid0, low[0], ROWS).astype(BF), mm(resid1, low[1], ROWS).astype(BF)])
    return dec, enc, enc_bias, bias_grad


def solution(mesh):
    return jax.shard_map(
        per_device,
        mesh=mesh,
        in_specs=(
            P(None, ("grp", "layer"), None),
            P(None, ("grp", "layer"), None),
            P(None, ("grp", "layer"), None, None),
            P(None, ("grp", "layer"), None),
            P(None, "layer", None),
            P(),
        ),
        out_specs=(
            P("grp", "layer", None),
            P("grp", None, "layer"),
            P("grp", "layer"),
            P("grp", None),
        ),
        check_vma=False,
    )
```

```python
import math

import jax
import jax.numpy as jnp
from jax import lax
from jax.experimental import pallas as pl
from jax.experimental.pallas import tpu as pltpu
from jax.sharding import PartitionSpec as P

BF = jnp.bfloat16
F32 = jnp.float32
ROWS = ((0,), (0,))
LAST = ((1,), (1,))
SMALL = pl.CostEstimate(flops=1, bytes_accessed=1, transcendentals=0)
PARAMS = pltpu.CompilerParams(vmem_limit_bytes=56 * 2**20)


def mm(a, b, dims=((1,), (0,))):
    return lax.dot_general(a, b, (dims, ((), ())), preferred_element_type=F32)


def column_block(width):
    return next((b for b in (896, 512, 256, 128) if width % b == 0), width)


def first_rows(routes, target, pre, groups, cap):
    layers, tokens, width = target.shape
    latents = pre.shape[2]
    slots = groups * cap
    step = column_block(width)

    def kernel(routes_ref, target_ref, pre_ref, out_ref, order_ref):
        at = lax.broadcasted_iota(jnp.int32, (tokens, tokens), 0)
        earlier = at < lax.broadcasted_iota(jnp.int32, (tokens, tokens), 1)
        slot = lax.broadcasted_iota(jnp.int32, (slots, tokens), 0)
        hot = []
        for l in range(layers):
            named = routes_ref[l : l + 1, :]
            other = jnp.broadcast_to(named.astype(F32), (tokens, tokens)).T
            same = earlier & (other == named.astype(F32))
            order = jnp.sum(same.astype(F32), axis=0, keepdims=True).astype(jnp.int32)
            order_ref[l : l + 1, :] = order
            hot.append((named * cap + order == slot).astype(F32).astype(BF))
        for i in range(width // step):
            cols = slice(i * step, (i + 1) * step)
            out_ref[:, cols] = mm(hot[0], target_ref[0, :, cols]).astype(BF)
        for l in range(layers):
            cols = slice(width + l * latents, width + (l + 1) * latents)
            out_ref[:, cols] = mm(hot[l], pre_ref[l]).astype(BF)

    whole = lambda shape: pl.BlockSpec(shape, lambda i: (0,) * len(shape))
    return pl.pallas_call(
        kernel,
        grid=(1,),
        in_specs=[
            whole((layers, tokens)),
            whole((1, tokens, width)),
            whole((layers, tokens, latents)),
        ],
        out_specs=[whole((slots, width + layers * latents)), whole((layers, tokens))],
        out_shape=[
            jax.ShapeDtypeStruct((slots, width + layers * latents), BF),
            jax.ShapeDtypeStruct((layers, tokens), jnp.int32),
        ],
        compiler_params=PARAMS,
        cost_estimate=SMALL,
    )(routes, target, pre)


def decoded_pieces(base, first, decoder, half, cap):
    _, latents, width = decoder.shape
    slots = first.shape[0]
    rows = half * cap
    step = column_block(width)

    def kernel(base_ref, pre_ref, dec1_ref, dec2_ref, far_ref, near_ref):
        for at, out_ref in enumerate((near_ref, far_ref)):
            begin = pl.multiple_of(base_ref[at], rows)
            for l, dec_ref in enumerate((dec1_ref, dec2_ref)):
                pre = pre_ref[pl.ds(begin, rows), l * latents : (l + 1) * latents]
                act = jnp.maximum(pre.astype(F32), 0).astype(BF)
                piece = mm(act, dec_ref[0]).astype(BF)
                for j in range(half):
                    place = (2 * j + l) * cap
                    out_ref[place : place + cap, :] = piece[j * cap : (j + 1) * cap]

    return pl.pallas_call(
        kernel,
        grid=(width // step,),
        in_specs=[
            pl.BlockSpec(memory_space=pltpu.SMEM),
            pl.BlockSpec((slots, 2 * latents), lambda i: (0, width // (2 * latents))),
            pl.BlockSpec((1, latents, step), lambda i: (1, 0, i)),
            pl.BlockSpec((1, latents, step), lambda i: (2, 0, i)),
        ],
        out_specs=[pl.BlockSpec((2 * rows, step), lambda i: (0, i))] * 2,
        out_shape=[jax.ShapeDtypeStruct((2 * rows, width), BF)] * 2,
        compiler_params=PARAMS,
        cost_estimate=SMALL,
    )(base, first, decoder, decoder)


def pack_rows(keys, rows, groups, cap):
    layers, tokens, width = rows.shape
    step = column_block(width)

    def kernel(keys_ref, rows_ref, *outs):
        slot = lax.broadcasted_iota(jnp.int32, (groups * cap, tokens), 0)
        for l in range(layers):
            hot = (keys_ref[l : l + 1, :] == slot).astype(F32).astype(BF)
            placed = mm(hot, rows_ref[l]).astype(BF)
            for k in range(groups):
                outs[k][l * cap : (l + 1) * cap, :] = placed[k * cap : (k + 1) * cap]

    return pl.pallas_call(
        kernel,
        grid=(width // step,),
        in_specs=[
            pl.BlockSpec((layers, tokens), lambda i: (0, 0)),
            pl.BlockSpec((layers, tokens, step), lambda i: (0, 0, i)),
        ],
        out_specs=[pl.BlockSpec((layers * cap, step), lambda i: (0, i))] * groups,
        out_shape=[jax.ShapeDtypeStruct((layers * cap, width), BF)] * groups,
        compiler_params=PARAMS,
        cost_estimate=SMALL,
    )(keys, rows)


def layer0_errors(first, act, decoder, bias, scale):
    slots, latents = act.shape
    layers, width = bias.shape
    step = column_block(width)

    def kernel(act_ref, dec_ref, bias_ref, target_ref, sum_ref, grad_ref, back_ref):
        piece = mm(act_ref[...], dec_ref[0]).astype(BF).astype(F32)
        error = (piece + bias_ref[0:1, :] - target_ref[...].astype(F32)) * scale
        error = error.astype(BF)
        sum_ref[...] = jnp.sum(error.astype(F32), axis=0, keepdims=True)
        grad_ref[...] = mm(act_ref[...], error, ROWS).astype(BF)

        @pl.when(pl.program_id(0) == 0)
        def _():
            back_ref[...] = jnp.zeros_like(back_ref)

        back_ref[...] += mm(error, dec_ref[0], LAST)

    return pl.pallas_call(
        kernel,
        grid=(width // step,),
        in_specs=[
            pl.BlockSpec((slots, latents), lambda i: (0, 0)),
            pl.BlockSpec((1, latents, step), lambda i: (0, 0, i)),
            pl.BlockSpec((layers, step), lambda i: (0, i)),
            pl.BlockSpec((slots, step), lambda i: (0, i)),
        ],
        out_specs=[
            pl.BlockSpec((1, step), lambda i: (0, i)),
            pl.BlockSpec((latents, step), lambda i: (0, i)),
            pl.BlockSpec((slots, latents), lambda i: (0, 0)),
        ],
        out_shape=[
            jax.ShapeDtypeStruct((1, width), F32),
            jax.ShapeDtypeStruct((latents, width), BF),
            jax.ShapeDtypeStruct((slots, latents), F32),
        ],
        compiler_params=PARAMS,
        cost_estimate=SMALL,
    )(act, decoder, bias, first)


def gradients(me, errors, wide, decoder, pres, own, dec0, cap):
    devices = pres.shape[0]
    half = devices // 2
    pairs, latents, width = decoder.shape
    slots = devices * cap
    step = 2 * column_block(width)
    step = step if width % step == 0 else width
    steps = width // step

    def kernel(me_ref, eo_ref, em_ref, wo_ref, wm_ref, dec1_ref, dec2_ref, pre_ref, own_ref, dec0_ref, dec_ref, low_ref, bias_ref, back):
        at = pl.program_id(0)
        grad = mm(wo_ref[...], eo_ref[...], ROWS) + mm(wm_ref[...], em_ref[...], ROWS)
        dec_ref[0] = dec0_ref[...]
        dec_ref[1] = grad[:latents].astype(BF)
        dec_ref[2] = grad[latents:].astype(BF)

        @pl.when(at == 0)
        def _():
            back[...] = jnp.zeros_like(back)

        both = jnp.concatenate([dec1_ref[0], dec2_ref[0]], axis=0)
        back[0] += mm(eo_ref[...], both, LAST)
        back[1] += mm(em_ref[...], both, LAST)

        @pl.when(at == steps - 1)
        def _():
            my = me_ref[0]
            sums = [jnp.zeros((1, latents), F32) for _ in range(2)]
            for k in range(devices):
                group = (my ^ k) % half
                sender = my ^ k
                for l in range(2):
                    at_row = pl.multiple_of(group * 2 * cap + l * cap, cap)
                    part = back[k // half, pl.ds(at_row, cap), l * latents : (l + 1) * latents]
                    if l == 0:
                        part = part + own_ref[pl.ds(pl.multiple_of(sender * cap, cap), cap), :]
                    pre = pre_ref[(k // half) * half + group, l * cap : (l + 1) * cap, :]
                    part = jnp.where(pre.astype(F32) > 0, part, 0.0)
                    sums[l] = sums[l] + jnp.sum(part, axis=0, keepdims=True)
                    low_ref[l, k * cap : (k + 1) * cap, :] = part.astype(BF)
            for l in range(2):
                bias_ref[l : l + 1, :] = sums[l]

    whole = lambda shape: pl.BlockSpec(shape, lambda i: (0,) * len(shape))
    return pl.pallas_call(
        kernel,
        grid=(steps,),
        in_specs=[pl.BlockSpec(memory_space=pltpu.SMEM)]
        + [pl.BlockSpec((half * 2 * cap, step), lambda i: (0, i))] * 2
        + [whole((half * 2 * cap, 2 * latents))] * 2
        + [
            pl.BlockSpec((1, latents, step), lambda i: (1, 0, i)),
            pl.BlockSpec((1, latents, step), lambda i: (2, 0, i)),
            whole((devices, 2 * cap, latents)),
            whole((slots, latents)),
            pl.BlockSpec((latents, step), lambda i: (0, i)),
        ],
        out_specs=[
            pl.BlockSpec((pairs, latents, step), lambda i: (0, 0, i)),
            whole((2, slots, latents)),
            whole((2, latents)),
        ],
        out_shape=[
            jax.ShapeDtypeStruct((pairs, latents, width), BF),
            jax.ShapeDtypeStruct((2, slots, latents), BF),
            jax.ShapeDtypeStruct((2, latents), F32),
        ],
        scratch_shapes=[pltpu.VMEM((2, half * 2 * cap, 2 * latents), F32)],
        compiler_params=PARAMS,
        cost_estimate=SMALL,
    )(me, *errors, *wide, decoder, decoder, pres, own, dec0)


def encoder_products(resid, low, cap):
    devices = len(resid)
    _, slots, latents = low.shape
    width = resid[0].shape[1]
    step = column_block(width)

    def kernel(low_ref, *refs):
        rows, enc_ref, all_rows = refs[:devices], refs[devices], refs[devices + 1]
        for l in range(2):
            for k in range(devices):
                all_rows[l, k * cap : (k + 1) * cap, :] = rows[k][l * cap : (l + 1) * cap, :]
            enc_ref[l] = mm(all_rows[l], low_ref[l], ROWS).astype(BF)

    return pl.pallas_call(
        kernel,
        grid=(width // step,),
        in_specs=[pl.BlockSpec((2, slots, latents), lambda i: (0, 0, 0))]
        + [pl.BlockSpec((2 * cap, step), lambda i: (0, i))] * devices,
        out_specs=pl.BlockSpec((2, step, latents), lambda i: (0, i, 0)),
        out_shape=jax.ShapeDtypeStruct((2, width, latents), BF),
        scratch_shapes=[pltpu.VMEM((2, slots, step), BF)],
        compiler_params=PARAMS,
        cost_estimate=SMALL,
    )(low, *resid)


def per_device(residual, mlp_target, pre_acts, blocks, decoder, decoder_bias):
    devices = lax.axis_size("layer")
    layers, tokens, width = residual.shape
    latents = pre_acts.shape[3]
    cap = max(2, 2 * tokens // devices)
    slots = devices * cap
    half = devices // 2
    scale = 1.0 / math.sqrt(tokens)
    me = lax.axis_index("layer")
    upper = me >= half
    mirror = [(i, (i + half) % devices) for i in range(devices)]
    halves = [list(range(half)), list(range(half, devices))]

    def everyone(x):
        return lax.all_to_all(x, "layer", split_axis=0, concat_axis=0, tiled=True)

    def within(x):
        return lax.all_to_all(
            x, "layer", split_axis=0, concat_axis=0, tiled=True, axis_index_groups=halves
        )

    def after(x, done):
        return lax.optimization_barrier((x, done))[0]

    def across(x):
        return lax.ppermute(x, "layer", mirror)

    def turn(x):
        first, second = x[: x.shape[0] // 2], x[x.shape[0] // 2 :]
        return jnp.concatenate(
            [jnp.where(upper, second, first), jnp.where(upper, first, second)], axis=0
        )

    routes = blocks.reshape(layers, tokens)
    pre = pre_acts.reshape(layers, tokens, latents)
    direct = devices == 16 and cap % 16 == 0
    if direct:
        first, order = first_rows(routes, mlp_target, pre, devices, cap)
    else:
        earlier = jnp.arange(tokens)[:, None] > jnp.arange(tokens)[None, :]
        same = routes[:, :, None] == routes[:, None, :]
        order = jnp.sum((same & earlier).astype(jnp.int32), axis=2)
        slot_of = (routes * cap + order)[:, None, :]
        place = (slot_of == jnp.arange(slots, dtype=jnp.int32)[None, :, None]).astype(BF)
        first = jnp.concatenate(
            [
                mm(place[0], mlp_target[0]).astype(BF),
                mm(place[0], pre[0]).astype(BF),
                mm(place[1], pre[1]).astype(BF),
            ],
            axis=1,
        )
    routes_m, order_m = across(jnp.stack([routes, order]))

    def pair_places(named, order, base):
        block = base + jnp.arange(half, dtype=jnp.int32)[:, None, None, None]
        slot = jnp.arange(cap, dtype=jnp.int32)[None, None, :, None]
        hit = (named[None, :, None, :] == block) & (order[None, :, None, :] == slot)
        return hit.astype(BF).reshape(half, layers, cap, tokens)

    base = jnp.where(upper, half, 0).astype(jnp.int32)
    place_o = pair_places(routes, order, base)
    place_m = pair_places(routes_m, order_m, base)

    def flat(p):
        return p.reshape(-1, p.shape[-1])

    first = everyone(first.reshape(devices, cap, -1)).reshape(slots, -1)
    pre0 = first[:, width : width + latents]
    pre1 = first[:, width + latents :]
    act0 = jnp.maximum(pre0, 0)
    got_pre = jnp.stack(
        [pre0.reshape(devices, cap, latents), pre1.reshape(devices, cap, latents)], axis=1
    )

    later = half + half // 2
    windows = [
        list(range(1, half - 2)),
        list(range(half, later)),
        [half - 2],
        [half - 1],
        list(range(later, devices)),
    ]
    arrivals = [None] * devices
    if direct:
        packed = pack_rows((routes ^ me) * cap + order, residual, devices, cap)
        arrivals[0] = packed[0]

    def depart(window, begin):
        if not direct:
            return
        rows = [packed[k] for k in windows[window]]
        if begin is not None:
            rows = after(rows, begin)
        for k, x in zip(windows[window], rows):
            arrivals[k] = lax.ppermute(x, "layer", [(i, i ^ k) for i in range(devices)])

    def arrived(window):
        return [arrivals[k] for k in windows[window]] if direct else []

    acts = turn(jnp.maximum(got_pre, 0))
    nothing = jnp.zeros((devices, 1, cap, latents), BF)
    wide = jnp.concatenate(
        [
            jnp.concatenate([acts[:, 0:1], nothing], axis=3),
            jnp.concatenate([nothing, acts[:, 1:2]], axis=3),
        ],
        axis=1,
    ).reshape(devices, layers * cap, 2 * latents)
    dec1 = decoder[1:3].reshape(2 * latents, width)

    def decode(rows):
        return mm(rows.reshape(-1, 2 * latents), dec1).astype(BF).reshape(half, -1, width)

    depart(0, None)
    depart(1, got_pre)
    if direct:
        bases = jnp.stack([base * cap, (half - base) * cap]).astype(jnp.int32)
        pieces_m, pieces_o = (
            x.reshape(half, -1, width) for x in decoded_pieces(bases, first, decoder, half, cap)
        )
    else:
        pieces_m, pieces_o = decode(wide[half:]), decode(wide[:half])
    pieces_m = within(after(pieces_m, (arrived(0), routes_m))).reshape(-1, width)
    sum_m = mm(flat(place_m), pieces_m, ROWS).astype(BF)
    sum_low = across(sum_m)
    depart(2, sum_m)
    pieces_o = within(after(pieces_o, (sum_m, arrived(1)))).reshape(-1, width)
    sum0, dec0, own = layer0_errors(
        after(first, sum_m), act0, decoder, decoder_bias, scale
    )
    empty0 = (decoder_bias[0] * scale).astype(BF).astype(F32)
    empties = float(slots * devices - tokens * devices)

    pieces_o = after(pieces_o, sum0)
    sum_o = mm(flat(place_o), pieces_o, ROWS) + decoder_bias[1] - mlp_target[1].astype(F32)
    sum_o = lax.optimization_barrier(sum_o.astype(BF))
    head = 16 if direct else tokens // 2
    sum_high_head = across(sum_o[:head])
    depart(3, sum_o)

    def add_halves(a, b):
        return ((a.astype(F32) + b.astype(F32)) * scale).astype(BF)

    def sent(x, step):
        return lax.ppermute(x, "layer", [(i, i ^ step) for i in range(devices)])

    error1 = add_halves(sum_o, sum_low)
    sums = jnp.concatenate([sum0, jnp.sum(error1.astype(F32), axis=0, keepdims=True)])
    sent_o = mm(flat(place_o), error1).astype(BF).reshape(half, layers * cap, width)
    sent_o, rest = after((sent_o, sum_o[head:]), (sum_high_head, arrived(2)))
    errors_o = within(sent_o).reshape(-1, width)
    sum_high = jnp.concatenate([sum_high_head, across(rest)])
    sums = after(sums, errors_o)
    step = devices // 2
    while step > 2:
        if direct and step == 8:
            sums = (sums + sent(sums, 4)) + (sent(sums, 8) + sent(sums, 12))
            step = 2
        else:
            sums = sums + sent(sums, step)
            step //= 2
    error1_m = after(add_halves(sum_m, sum_high), (errors_o, arrived(3)))
    sent_errors = mm(flat(place_m), error1_m).astype(BF).reshape(half, layers * cap, width)
    sent_errors = after(sent_errors, sums)
    depart(4, sent_errors)
    errors_m = within(sent_errors).reshape(-1, width)
    if devices > 1:
        sums = sums + sent(after(sums, sent_errors), 1)
    errors_m = after(errors_m, sums)
    if devices > 2:
        sums = sums + sent(sums, 2)
    bias_grad = sums - jnp.stack([empties * empty0, jnp.zeros_like(empty0)])

    wide_o = wide[:half].reshape(-1, 2 * latents)
    wide_m = wide[half:].reshape(-1, 2 * latents)
    if direct:
        pres = turn(got_pre).reshape(devices, layers * cap, latents)
        dec, low, enc_bias = gradients(
            me.astype(jnp.int32).reshape(1),
            (errors_o, errors_m),
            (wide_o, wide_m),
            decoder,
            pres,
            own,
            dec0,
            cap,
        )
        enc = encoder_products(after(arrivals, low), low, cap)
    else:
        resid = everyone(
            jnp.stack(
                [
                    mm(place[l], residual[l]).astype(BF).reshape(devices, cap, width)
                    for l in range(layers)
                ],
                axis=1,
            ).reshape(devices, layers * cap, width)
        ).reshape(devices, layers, cap, width)
        dec_later = mm(wide_o, errors_o, ROWS) + mm(wide_m, errors_m, ROWS)
        dec = jnp.concatenate([dec0[None], dec_later.astype(BF).reshape(2, latents, width)])
        back = jnp.concatenate([mm(errors_o, dec1, LAST), mm(errors_m, dec1, LAST)], axis=0)
        back = turn(back.reshape(devices, layers, cap, 2 * latents))
        own = own.reshape(devices, cap, latents)
        grads = jnp.stack([back[:, 0, :, :latents] + own, back[:, 1, :, latents:]])
        grads = jnp.where(jnp.swapaxes(got_pre, 0, 1) > 0, grads, 0.0)
        grads = grads.reshape(layers, slots, latents)
        enc_bias = jnp.sum(grads, axis=1)
        resid = jnp.swapaxes(resid, 0, 1).reshape(layers, slots, width)
        enc = jnp.stack([mm(resid[l], grads[l].astype(BF), ROWS).astype(BF) for l in range(layers)])
    return dec, enc, enc_bias, bias_grad


def solution(mesh):
    return jax.shard_map(
        per_device,
        mesh=mesh,
        in_specs=(
            P(None, ("grp", "layer"), None),
            P(None, ("grp", "layer"), None),
            P(None, ("grp", "layer"), None, None),
            P(None, ("grp", "layer"), None),
            P(None, "layer", None),
            P(),
        ),
        out_specs=(
            P("grp", "layer", None),
            P("grp", None, "layer"),
            P("grp", "layer"),
            P("grp", None),
        ),
        check_vma=False,
    )
```
